128 devices in a mesh: seq: 32 (over y_lo, z, x), head: 4 (over y_hi, core).
Axes of the slice: x: 4, y: 4 (y_hi: 2, y_lo: 2; y = y_hi * 2 + y_lo), z: 4, core: 2. Of those that a mesh axis runs over, the one named last changes fastest.
Arguments:
- prompt_q: bfloat16 [2, 2048, 8192], P(None, 'seq', 'head'), may hold values from -120 to 120
- prompt_k: bfloat16 [2, 2048, 1024], P(None, 'seq', 'head'), may hold values from -6 to 6
- prompt_v: bfloat16 [2, 2048, 1024], P(None, 'seq', 'head'), may hold values from -6 to 6
- resp_q: bfloat16 [8192, 8192], P('seq', 'head'), may hold values from -120 to 120
- resp_k: bfloat16 [8192, 1024], P('seq', 'head'), may hold values from -6 to 6
- resp_v: bfloat16 [8192, 1024], P('seq', 'head'), may hold values from -6 to 6
- slot_resp: int32 [64], P('seq'), may hold values from 0 to 1, as said below
- resp_len: int32 [32], P('seq'), may hold values from 1 to 2, as said below
- resp_prompt: int32 [32], P('seq'), may hold values from 0 to 1, as said below
- d_prompt_out: bfloat16 [2, 2048, 8192], P(None, ('seq', 'head')), may hold values from -6 to 6
- d_resp_out: bfloat16 [8192, 8192], P(('seq', 'head')), may hold values from -6 to 6
Outputs:
- prompt_out: float32 [2, 2048, 8192], P(None, ('seq', 'head'))
- resp_out: float32 [8192, 8192], P(('seq', 'head'))
- d_prompt_q: float32 [2, 2048, 8192], P(None, 'seq', 'head')
- d_prompt_k: float32 [2, 2048, 1024], P(None, 'seq', 'head')
- d_prompt_v: float32 [2, 2048, 1024], P(None, 'seq', 'head')
- d_resp_q: float32 [8192, 8192], P('seq', 'head')
- d_resp_k: float32 [8192, 1024], P('seq', 'head')
- d_resp_v: float32 [8192, 1024], P('seq', 'head')
The draws below stay inside these ranges and needn't reach their ends.
Inputs may be any that keep to these rules, and one draw needn't show every extreme that they name: `slot_resp`: entry d * 2 + j names the local response of device d whose next block sits in slot j, or no response when it is 1; each local response has at least one slot; in every draw some device has all 2 slots live. `resp_len`: at most the number of slots that name the response on its device; the slots beyond it are padding. `resp_prompt`: each prompt is named by exactly 16 responses.
All inputs are finite; a program needn't handle non-finite values.
Results may differ from the reference program's by a relative error of at most 0.015.
Values may be sent and summed in bfloat16 or wider, within the bound.
No kernel may reach another device: no remote copies, remote signals or barrier semaphores. Data moves between devices by JAX's collectives and lax.ppermute only.
A program may use at most 128 MiB of HBM per device.

```python
import jax
import jax.numpy as jnp
from jax import lax

HD = 128
QH = 64
KVH = 8
BLK = 128
RDEV = 1
SLOTS = 2
PROMPTS = 2
PLEN = 2048
RESP = 32
RTOK = 8192
N_SEQ = 32


def paired_rows(key, row_total, width):
    fresh_rows = jnp.clip(jax.random.normal(key, (row_total // 2, 2, width), jnp.float32), -6.0, 6.0)
    second = jnp.clip(fresh_rows[:, 1], -6.0, 6.0)
    return jnp.stack([fresh_rows[:, 0], second], axis=1).reshape(row_total, width)


def prompt_key_rows(key):
    return paired_rows(jax.random.fold_in(key, 11), PROMPTS * PLEN, KVH * HD)


def resp_key_rows(key):
    return paired_rows(jax.random.fold_in(key, 12), RTOK, KVH * HD)


def slot_plan(key):
    subkeys = jax.random.split(jax.random.fold_in(key, 21), 5)
    slot_order = jnp.arange(SLOTS, dtype=jnp.int32)
    members = jnp.arange(RDEV, dtype=jnp.int32)

    def device_order(device_key):
        return jax.random.permutation(device_key, SLOTS)
    orders = jax.vmap(device_order)(jax.random.split(subkeys[0], N_SEQ))
    forced = orders[:, None, :RDEV] == slot_order[None, :, None]
    chosen = jnp.any(forced, axis=2)
    forced_value = jnp.sum(jnp.where(forced, members[None, None, :], 0), axis=2)
    random_slot = jax.random.randint(subkeys[1], (N_SEQ, SLOTS), 0, RDEV + 1)
    slot_table = jnp.where(chosen, forced_value, random_slot)
    allocated = jnp.sum((slot_table[:, :, None] == members[None, None, :]).astype(jnp.int32), axis=1)
    first_draw = jax.random.randint(subkeys[2], (N_SEQ, RDEV), 0, allocated)
    second_draw = jax.random.randint(subkeys[3], (N_SEQ, RDEV), 0, allocated)
    lengths = 1 + jnp.minimum(first_draw, second_draw)
    full_device = jax.random.randint(subkeys[4], (), 0, N_SEQ)
    full_slots = jnp.where(slot_order < SLOTS - RDEV + 1, 0, slot_order - (SLOTS - RDEV))
    full_lengths = jnp.where(members == 0, SLOTS - RDEV + 1, 1)
    is_full = jnp.arange(N_SEQ, dtype=jnp.int32)[:, None] == full_device
    slot_table = jnp.where(is_full, full_slots[None, :], slot_table)
    lengths = jnp.where(is_full, full_lengths[None, :], lengths)
    return (slot_table.reshape(-1).astype(jnp.int32), lengths.reshape(-1).astype(jnp.int32))


def draw_prompt_k(key, part):
    return prompt_key_rows(key).reshape(PROMPTS, PLEN, KVH * HD).astype(jnp.bfloat16)


def draw_resp_k(key, part):
    return resp_key_rows(key).astype(jnp.bfloat16)


def draw_prompt_q(key, part):
    key = jax.random.fold_in(key, 3)
    fresh_rows = jnp.clip(jax.random.normal(key, (PROMPTS * PLEN, QH * HD), jnp.float32), -6.0, 6.0)
    return fresh_rows.reshape(PROMPTS, PLEN, QH * HD).astype(jnp.bfloat16)


def draw_resp_q(key, part):
    key = jax.random.fold_in(key, 4)
    fresh_rows = jnp.clip(jax.random.normal(key, (RTOK, QH * HD), jnp.float32), -6.0, 6.0)
    return fresh_rows.astype(jnp.bfloat16)


def draw_slot_resp(key, part):
    return slot_plan(key)[0]


def draw_resp_len(key, part):
    return slot_plan(key)[1]


def draw_resp_prompt(key, part):
    key = jax.random.fold_in(key, 31)
    return (jax.random.permutation(key, RESP) % PROMPTS).astype(jnp.int32)


def block_levels(key, shape, cuts, low, largest):
    gain = 1.0
    for dim, shards_of in cuts:
        steps = jax.random.uniform(jax.random.fold_in(jax.random.fold_in(key, 6), dim), (shards_of,), jnp.float32, low / len(cuts), largest / len(cuts))
        gain = gain * jnp.repeat(jnp.exp(steps), shape[dim] // shards_of).reshape((-1,) + (1,) * (len(shape) - 1 - dim))
    return gain


def scatter_about(key, extent, scale, bound, shards=(), held_as=jnp.bfloat16):
    entries = scale * jax.random.normal(key, extent, jnp.float32)
    if shards:
        entries = entries * block_levels(key, extent, shards, -0.22, 0.18)
    return jnp.clip(entries, -bound, bound).astype(held_as)


def setup_inputs(seed: int = 0) -> dict:
    splits = jax.random.split(jax.random.key(seed), 12)
    return {
        "prompt_q": draw_prompt_q(jax.random.fold_in(splits[11], 71), 0),
        "prompt_k": draw_prompt_k(jax.random.fold_in(splits[11], 71), 0),
        "prompt_v": scatter_about(splits[2], (PROMPTS, PLEN, KVH * HD), 1.0, 6.0, ((1, 32), (2, 4))),
        "resp_q": draw_resp_q(jax.random.fold_in(splits[11], 71), 0),
        "resp_k": draw_resp_k(jax.random.fold_in(splits[11], 71), 0),
        "resp_v": scatter_about(splits[5], (RTOK, KVH * HD), 1.0, 6.0, ((0, 32), (1, 4))),
        "slot_resp": draw_slot_resp(jax.random.fold_in(splits[11], 71), 0),
        "resp_len": draw_resp_len(jax.random.fold_in(splits[11], 71), 0),
        "resp_prompt": draw_resp_prompt(jax.random.fold_in(splits[11], 71), 0),
        "d_prompt_out": scatter_about(splits[9], (PROMPTS, PLEN, QH * HD), 1.0, 6.0, ((1, 128),)),
        "d_resp_out": scatter_about(splits[10], (RTOK, QH * HD), 1.0, 6.0, ((0, 128),)),
    }


neg_big = -1e30


def slot_info(slot_resp, resp_len, resp_prompt):
    slot_table = slot_resp.reshape(N_SEQ, SLOTS)
    slot_order = jnp.arange(SLOTS, dtype=jnp.int32)
    same_resp = slot_table[:, :, None] == slot_table[:, None, :]
    earlier = slot_order[None, None, :] < slot_order[None, :, None]
    slot_block = jnp.sum((same_resp & earlier).astype(jnp.int32), axis=2)
    member = jnp.minimum(slot_table, RDEV - 1)
    global_id = (jnp.arange(N_SEQ, dtype=jnp.int32)[:, None] * RDEV + member).astype(jnp.int32)
    slot_live = (slot_table < RDEV) & (slot_block < resp_len[global_id])
    slot_owner = jnp.where(slot_live, slot_table, -1)
    return slot_owner, slot_block, resp_prompt[global_id], slot_live


def attention_block(queries, key_rows, value_rows, d_out, allowed_keys):
    score_scale = HD ** -0.5
    queries32 = queries.astype(jnp.float32)
    keys32 = key_rows.astype(jnp.float32)
    values32 = value_rows.astype(jnp.float32)
    d_out32 = d_out.astype(jnp.float32)
    scores = jnp.einsum('bajd,bnd->bajn', queries32, keys32) * score_scale
    allowed = allowed_keys[:, :, None, :]
    masked = jnp.where(allowed, scores, neg_big)
    row_max = jnp.max(masked, axis=-1)
    row_sum = jnp.sum(jnp.where(allowed, jnp.exp(masked - row_max[..., None]), 0.0), axis=-1)
    has_keys = jnp.any(allowed_keys, axis=-1)[:, :, None]
    log_total = jnp.where(has_keys, row_max + jnp.log(jnp.where(has_keys, row_sum, 1.0)), 0.0)
    weights = jnp.where(allowed, jnp.exp(masked - log_total[..., None]), 0.0)
    weights_half = lax.optimization_barrier(weights.astype(jnp.bfloat16)).astype(jnp.float32)
    output = jnp.einsum('bajn,bnd->bajd', weights_half, values32)
    row_delta = jnp.sum(d_out32 * output, axis=-1)
    d_weights = jnp.einsum('bajd,bnd->bajn', d_out32, values32)
    d_scores = lax.optimization_barrier((weights * (d_weights - row_delta[..., None])).astype(jnp.bfloat16)).astype(jnp.float32)
    d_queries = score_scale * jnp.einsum('bajn,bnd->bajd', d_scores, keys32)
    d_keys = score_scale * jnp.einsum('bajn,bajd->bnd', d_scores, queries32)
    d_values = jnp.einsum('bajn,bajd->bnd', weights_half, d_out32)
    return output, d_queries, d_keys, d_values


def prompt_part(prompt_q, prompt_k, prompt_v, d_prompt_out):
    group_size = QH // KVH
    q_heads = prompt_q.reshape(PROMPTS, PLEN, KVH, group_size, HD).transpose(2, 0, 1, 3, 4)
    k_heads = prompt_k.reshape(PROMPTS, PLEN, KVH, HD).transpose(2, 0, 1, 3)
    v_heads = prompt_v.reshape(PROMPTS, PLEN, KVH, HD).transpose(2, 0, 1, 3)
    do_heads = d_prompt_out.reshape(PROMPTS, PLEN, KVH, group_size, HD).transpose(2, 0, 1, 3, 4)
    positions = jnp.arange(PLEN, dtype=jnp.int32)
    causal = jnp.broadcast_to((positions[None, :] <= positions[:, None])[None], (PROMPTS, PLEN, PLEN))

    def one_head(head_items):
        queries, key_rows, value_rows, d_out = head_items
        return attention_block(queries, key_rows, value_rows, d_out, causal)

    return lax.map(one_head, (q_heads, k_heads, v_heads, do_heads))


def reference(prompt_q, prompt_k, prompt_v, resp_q, resp_k, resp_v, slot_resp, resp_len, resp_prompt, d_prompt_out, d_resp_out):
    group_size = QH // KVH
    slot_rows = SLOTS * BLK
    slot_owner, slot_block, slot_prompt, slot_live = slot_info(slot_resp, resp_len, resp_prompt)
    p_out, p_dq, p_dk, p_dv = prompt_part(prompt_q, prompt_k, prompt_v, d_prompt_out)
    pk_heads = prompt_k.reshape(PROMPTS, PLEN, KVH, HD).transpose(2, 0, 1, 3)
    pv_heads = prompt_v.reshape(PROMPTS, PLEN, KVH, HD).transpose(2, 0, 1, 3)

    def one_device(folded, device_items):
        queries, key_rows, value_rows, d_out, dev_owner, dev_block, dev_prompt, dev_live = device_items
        tok_owner = jnp.repeat(dev_owner, BLK)
        tok_pos = (dev_block[:, None] * BLK + jnp.arange(BLK, dtype=jnp.int32)[None, :]).reshape(slot_rows)
        self_mask = (tok_owner[:, None] == tok_owner[None, :]) & (tok_owner[:, None] >= 0) & (tok_pos[None, :] <= tok_pos[:, None])
        prompt_mask = jnp.broadcast_to(dev_live[:, None, None], (SLOTS, BLK, PLEN))
        allowed_keys = jnp.concatenate([prompt_mask, self_mask.reshape(SLOTS, BLK, slot_rows)], axis=2)
        slot_pick = (dev_prompt[:, None] == jnp.arange(PROMPTS, dtype=jnp.int32)[None, :]).astype(jnp.float32)
        q_heads = queries.reshape(SLOTS, BLK, KVH, group_size, HD).transpose(2, 0, 1, 3, 4)
        k_heads = key_rows.reshape(slot_rows, KVH, HD).transpose(1, 0, 2)
        v_heads = value_rows.reshape(slot_rows, KVH, HD).transpose(1, 0, 2)
        do_heads = d_out.reshape(SLOTS, BLK, KVH, group_size, HD).transpose(2, 0, 1, 3, 4)

        def one_head(head_items):
            head_q, head_k, head_v, head_do, head_pk, head_pv = head_items
            near_k = head_pk[dev_prompt]
            near_v = head_pv[dev_prompt]
            all_k = jnp.concatenate([near_k, jnp.broadcast_to(head_k[None], (SLOTS, slot_rows, HD))], axis=1)
            all_v = jnp.concatenate([near_v, jnp.broadcast_to(head_v[None], (SLOTS, slot_rows, HD))], axis=1)
            output, d_queries, d_keys, d_values = attention_block(head_q, all_k, all_v, head_do, allowed_keys)
            pk_grad = jnp.einsum('sp,snd->pnd', slot_pick, d_keys[:, :PLEN], precision=lax.Precision.HIGHEST)
            pv_grad = jnp.einsum('sp,snd->pnd', slot_pick, d_values[:, :PLEN], precision=lax.Precision.HIGHEST)
            return output, d_queries, jnp.sum(d_keys[:, PLEN:], axis=0), jnp.sum(d_values[:, PLEN:], axis=0), pk_grad, pv_grad

        output, d_queries, key_self, value_self, pk_grad, pv_grad = lax.map(one_head, (q_heads, k_heads, v_heads, do_heads, pk_heads, pv_heads))
        folded = (folded[0] + pk_grad, folded[1] + pv_grad)
        out_rows = output.transpose(1, 2, 0, 3, 4).reshape(slot_rows, QH * HD)
        dq_rows = d_queries.transpose(1, 2, 0, 3, 4).reshape(slot_rows, QH * HD)
        dk_rows = key_self.transpose(1, 0, 2).reshape(slot_rows, KVH * HD)
        dv_rows = value_self.transpose(1, 0, 2).reshape(slot_rows, KVH * HD)
        return folded, (out_rows, dq_rows, dk_rows, dv_rows)

    zero_grads = jnp.zeros((KVH, PROMPTS, PLEN, HD), jnp.float32)
    device_items = (resp_q.reshape(N_SEQ, slot_rows, QH * HD), resp_k.reshape(N_SEQ, slot_rows, KVH * HD),
                    resp_v.reshape(N_SEQ, slot_rows, KVH * HD), d_resp_out.reshape(N_SEQ, slot_rows, QH * HD),
                    slot_owner, slot_block, slot_prompt, slot_live)
    (pk_total, pv_total), (r_out, r_dq, r_dk, r_dv) = lax.scan(one_device, (zero_grads, zero_grads), device_items)
    prompt_out = p_out.transpose(1, 2, 0, 3, 4).reshape(PROMPTS, PLEN, QH * HD)
    d_prompt_q = p_dq.transpose(1, 2, 0, 3, 4).reshape(PROMPTS, PLEN, QH * HD)
    d_prompt_k = (p_dk + pk_total).transpose(1, 2, 0, 3).reshape(PROMPTS, PLEN, KVH * HD)
    d_prompt_v = (p_dv + pv_total).transpose(1, 2, 0, 3).reshape(PROMPTS, PLEN, KVH * HD)
    resp_out = r_out.reshape(RTOK, QH * HD)
    d_resp_q = r_dq.reshape(RTOK, QH * HD)
    d_resp_k = r_dk.reshape(RTOK, KVH * HD)
    d_resp_v = r_dv.reshape(RTOK, KVH * HD)
    return (prompt_out, resp_out, d_prompt_q, d_prompt_k, d_prompt_v, d_resp_q, d_resp_k, d_resp_v)
```

```python
import math

import jax
import jax.numpy as jnp
from jax import lax
from jax.experimental import pallas as pl
from jax.experimental.pallas import tpu as pltpu
from jax.sharding import Mesh
from jax.sharding import PartitionSpec as P

BF = jnp.bfloat16
F4 = jnp.float32
HD = 128
G = 8
W = G * HD
KB = 512
RB = 512
NEG = -1e30
SCALE = HD**-0.5
C2 = SCALE * math.log2(math.e)
PARAMS = pltpu.CompilerParams(vmem_limit_bytes=56 * 2**20)
SEQ, LIVE, PROMPT, SOURCE = 1, 2, 4, 4


def nt(a, b):
    return lax.dot_general(a, b, (((1,), (1,)), ((), ())), preferred_element_type=F4)


def nn(a, b):
    return lax.dot_general(a, b, (((1,), (0,)), ((), ())), preferred_element_type=F4)


def cols(g):
    return slice(g * HD, (g + 1) * HD)


def kv_block(kv, which, p, j):
    ring = pl.multiple_of((j & 1) * 8, 8)
    return kv[pl.ds(ring, 8), j >> 1, which, p].reshape(KB, HD)


def causal_mask(seq, j):
    key = j * KB + lax.broadcasted_iota(jnp.int32, (KB, RB), 0)
    row = seq * 64 + (lax.broadcasted_iota(jnp.int32, (KB, RB), 1) & 63)
    return key <= row


def self_mask(j, live_0):
    key = lax.broadcasted_iota(jnp.int32, (256, RB), 0)
    row = j * 128 + (lax.broadcasted_iota(jnp.int32, (256, RB), 1) & 127)
    first = jnp.where(live_0 > 0, 0, j * 128)
    return (key >= first) & (key <= row)


def load_queries(qx, qp, qs, qr):
    for g in range(G):
        for p in range(2):
            at = pl.ds(g * 64, 64)
            qx[p, at, :] = qp[p, :, cols(g)]
            qx[6 + p, at, :] = qr[p * 64 : p * 64 + 64, cols(g)]
        for j in range(2):
            at = pl.ds((g % 4) * 128, 128)
            qx[2 + 2 * j + g // 4, at, :] = qs[j * 128 : j * 128 + 128, cols(g)]
            qx[8 + 2 * j + g // 4, at, :] = qr[128 + j * 128 : 256 + j * 128, cols(g)]


def load_own_pairs(kx, ks, vs, qr):
    for which, ref in ((0, ks), (1, vs)):
        kx[0, which] = ref[...]
        for n in range(4):
            kx[1, which, n * 64 : n * 64 + 64, :] = qr[384:448, cols(which * 4 + n)]


def step(k, q, vt, m, l, acc, mask=None):
    s = nt(k, q)
    if mask is not None:
        s = jnp.where(mask, s, NEG)
    top = jnp.maximum(m, jnp.max(s, 0, keepdims=True))
    p = jnp.exp2((s - top) * C2)
    fade = jnp.exp2((m - top) * C2)
    l = l * fade + jnp.sum(p, 0, keepdims=True)
    return top, l, acc * fade + nn(vt, p.astype(BF))


def fwd_kernel(info, kv, ks, vs, qp, qs, qr, o, ot, lse, vt, qx, kx, vst):
    load_queries(qx, qp, qs, qr)
    load_own_pairs(kx, ks, vs, qr)
    for p in range(2):
        for j in range(4):
            vt[p, j] = kv_block(kv, 1, p, j).T
    for b in range(2):
        vst[b] = kx[b, 1].T
    m0 = jnp.full((1, RB), NEG, F4)
    l0 = jnp.zeros((1, RB), F4)

    def finish(at, m, l, acc):
        acc = acc * (1.0 / l)
        ot[at] = acc
        lse[at] = m * C2 + jnp.log2(l)
        return acc.T.astype(BF)

    def prompts(b, carry):
        seq = info[SEQ + SOURCE * b]
        group = (info[0] ^ b) * 4
        last = seq >> 3
        for p in range(2):
            ot[6 * b + p] = jnp.zeros((HD, RB), F4)

        def body(j, c, masked=False):
            mask = causal_mask(seq, j) if masked else None
            out = []
            for p in range(2):
                m, l, acc = step(
                    kv_block(kv, 0, p, j), qx[6 * b + p], vt[p, j],
                    c[2 * p], c[2 * p + 1], ot[6 * b + p], mask,
                )
                ot[6 * b + p] = acc
                out += [m, l]
            return tuple(out)

        c = lax.fori_loop(0, last, body, (m0, l0, m0, l0))
        c = body(last, c, True)
        for p in range(2):
            rows = finish(6 * b + p, c[2 * p], c[2 * p + 1], ot[6 * b + p])
            for g in range(G):
                o[pl.ds(group, 4), p * 16 : p * 16 + 16, cols(g)] = rows[
                    g * 64 : g * 64 + 64
                ].reshape(4, 16, HD)
        return carry

    lax.fori_loop(0, 2, prompts, 0)

    def slots(n, carry):
        b, j = n >> 1, n & 1
        live = info[SEQ + SOURCE * b + 1 + j]
        live_0 = info[SEQ + SOURCE * b + 1]
        prompt = info[SEQ + SOURCE * b + 3]
        group = (info[0] ^ b) * 4 + 2 * j
        at = 6 * b + 2 + 2 * j

        @pl.when(live > 0)
        def _():
            state = [(m0, l0, jnp.zeros((HD, RB), F4))] * 2
            for kb in range(4):
                for h in range(2):
                    state[h] = step(
                        kv_block(kv, 0, prompt, kb), qx[at + h], vt[prompt, kb], *state[h]
                    )
            mask = self_mask(j, live_0)
            for h in range(2):
                rows = finish(at + h, *step(kx[b, 0], qx[at + h], vst[b], *state[h], mask=mask))
                for g in range(4):
                    o[pl.ds(group, 2), 32:96, cols(4 * h + g)] = rows[
                        g * 128 : g * 128 + 128
                    ].reshape(2, 64, HD)

        @pl.when(live == 0)
        def _():
            o[pl.ds(group, 2), 32:96, :] = jnp.zeros((2, 64, W), BF)

        return carry

    lax.fori_loop(0, 4, slots, 0)


def grads(k, v, q, do, kt, lse2, delta, mask=None):
    s = nt(k, q)
    dp = nt(v, do)
    e = s * C2 - lse2
    if mask is not None:
        e = jnp.where(mask, e, NEG)
    p = jnp.exp2(e)
    ds = (p * (dp - delta)).astype(BF)
    return nn(p.astype(BF), do), nn(ds, q), nn(kt, ds)


def bwd_kernel(
    info, kv, ks, vs, qp, qs, qr, do, ot, lse,
    tab, dqp, dqs, drk, drv, send, kt, qx, dx, kx, kst, dk, dv, dqt, dkx, dvx,
):
    load_queries(qx, qp, qs, qr)
    load_own_pairs(kx, ks, vs, qr)
    for b in range(2):
        group = (info[0] ^ b) * 4
        for g in range(G):
            for p in range(2):
                dx[6 * b + p, g * 64 : g * 64 + 64, :] = do[
                    pl.ds(group, 4), p * 16 : p * 16 + 16, cols(g)
                ].reshape(64, HD)
            for j in range(2):
                dx[6 * b + 2 + 2 * j + g // 4, (g % 4) * 128 : (g % 4) * 128 + 128, :] = do[
                    pl.ds(group + 2 * j, 2), 32:96, cols(g)
                ].reshape(128, HD)
        kst[b] = kx[b, 0].T
    for p in range(2):
        for j in range(4):
            kt[p, j] = kv_block(kv, 0, p, j).T
    for ref in (dk, dv, dkx, dvx):
        ref[...] = jnp.zeros_like(ref)

    def row_delta(at):
        return jnp.sum(dx[at].astype(F4).T * ot[at], 0, keepdims=True)

    def prompts(b, carry):
        seq = info[SEQ + SOURCE * b]
        last = seq >> 3
        delta = [row_delta(6 * b + p) for p in range(2)]
        for p in range(2):
            dqt[6 * b + p] = jnp.zeros((HD, RB), F4)

        def body(j, c, masked=False):
            mask = causal_mask(seq, j) if masked else None
            for p in range(2):
                at = 6 * b + p
                a_v, a_k, a_q = grads(
                    kv_block(kv, 0, p, j), kv_block(kv, 1, p, j), qx[at], dx[at], kt[p, j],
                    lse[at], delta[p], mask,
                )
                dv[p, j] += a_v
                dk[p, j] += a_k
                dqt[at] += a_q
            return c

        lax.fori_loop(0, last, body, 0)
        body(last, 0, True)
        return carry

    lax.fori_loop(0, 2, prompts, 0)

    def slots(n, carry):
        b, j = n >> 1, n & 1
        live = info[SEQ + SOURCE * b + 1 + j]
        live_0 = info[SEQ + SOURCE * b + 1]
        prompt = info[SEQ + SOURCE * b + 3]

        @pl.when(live > 0)
        def _():
            mask = self_mask(j, live_0)
            for h in range(2):
                at = 6 * b + 2 + 2 * j + h
                q, d, total = qx[at], dx[at], lse[at]
                delta = row_delta(at)
                acc = jnp.zeros((HD, RB), F4)
                for kb in range(4):
                    a_v, a_k, a_q = grads(
                        kv_block(kv, 0, prompt, kb), kv_block(kv, 1, prompt, kb), q, d,
                        kt[prompt, kb], total, delta,
                    )
                    dv[prompt, kb] += a_v
                    dk[prompt, kb] += a_k
                    acc = acc + a_q
                a_v, a_k, a_q = grads(kx[b, 0], kx[b, 1], q, d, kst[b], total, delta, mask)
                dvx[b] += a_v
                dkx[b] += a_k
                dqt[at] = acc + a_q

        @pl.when(live == 0)
        def _():
            for h in range(2):
                dqt[6 * b + 2 + 2 * j + h] = jnp.zeros((HD, RB), F4)

        return carry

    lax.fori_loop(0, 4, slots, 0)
    for b in range(2):
        for p in range(2):
            rows = (dqt[6 * b + p] * SCALE).T
            for g in range(G):
                part = rows[g * 64 : g * 64 + 64]
                if b == 0:
                    dqp[p, :, cols(g)] = part
                else:
                    send[p * 64 : p * 64 + 64, cols(g)] = part.astype(BF)
        for n in range(4):
            rows = (dqt[6 * b + 2 + n] * SCALE).T
            j, h = n // 2, n % 2
            for g in range(4):
                part = rows[g * 128 : g * 128 + 128]
                if b == 0:
                    dqs[j * 128 : j * 128 + 128, cols(4 * h + g)] = part
                else:
                    send[128 + j * 128 : 256 + j * 128, cols(4 * h + g)] = part.astype(BF)
    drk[...] = dkx[0] * SCALE
    drv[...] = dvx[0]
    for n in range(4):
        send[384:448, cols(n)] = (dkx[1, n * 64 : n * 64 + 64, :] * SCALE).astype(BF)
        send[384:448, cols(4 + n)] = dvx[1, n * 64 : n * 64 + 64, :].astype(BF)
    for p in range(2):
        for j in range(4):
            ring = (j & 1) * 8
            tab[ring : ring + 8, j >> 1, 0, p] = (dk[p, j] * SCALE).astype(BF).reshape(8, 64, HD)
            tab[ring : ring + 8, j >> 1, 1, p] = dv[p, j].astype(BF).reshape(8, 64, HD)


def whole(shape):
    return pl.BlockSpec(tuple(shape), lambda i, info: (0,) * len(shape))


def half_of(shape, other=0):
    lead = (0,) * (len(shape) - 1)
    return pl.BlockSpec(tuple(shape), lambda i, info: lead + (info[0] ^ other,))


ANY = pl.BlockSpec(memory_space=pl.ANY)


def call(kernel, info, ins, in_specs, outs, out_specs, scratch=(), grid=(1,), flops=0, aliases=None):
    name = kernel.__name__.replace("_kernel", "")
    return pl.pallas_call(
        kernel,
        grid_spec=pltpu.PrefetchScalarGridSpec(
            num_scalar_prefetch=1, grid=grid, in_specs=in_specs, out_specs=out_specs,
            scratch_shapes=list(scratch),
        ),
        out_shape=[jax.ShapeDtypeStruct(shape, dtype) for shape, dtype in outs],
        input_output_aliases=aliases or {},
        cost_estimate=pl.CostEstimate(
            flops=flops, bytes_accessed=4 * 10**6, transcendentals=flops // 1000
        ),
        compiler_params=PARAMS,
        name=name,
    )(info, *ins)


PACK = (384 + 64, W)
ROWS = [half_of((256, HD)), half_of((256, HD)), half_of((2, 64, W)), half_of((256, W)), whole(PACK)]
STATE = [((12, HD, RB), F4), ((12, 1, RB), F4)]


def fwd(info, kv, rows):
    return call(
        fwd_kernel, info, (kv, *rows), [whole(kv.shape), *ROWS],
        [((8, 96, W), BF), *STATE],
        [whole((8, 96, W)), *(whole(shape) for shape, _ in STATE)],
        [
            pltpu.VMEM((2, 4, HD, KB), BF), pltpu.VMEM((12, RB, HD), BF),
            pltpu.VMEM((2, 2, 256, HD), BF), pltpu.VMEM((2, HD, 256), BF),
        ],
        flops=2 * 10**10,
    )


def bwd(info, kv, rows, cot, out_t, lse):
    return call(
        bwd_kernel, info, (kv, *rows, cot, out_t, lse),
        [whole(kv.shape), *ROWS, whole(cot.shape), *(whole(shape) for shape, _ in STATE)],
        [
            (kv.shape, BF), ((2, 64, 2 * W), F4), ((256, 2 * W), F4),
            ((256, 2 * HD), F4), ((256, 2 * HD), F4), (PACK, BF),
        ],
        [
            whole(kv.shape), half_of((2, 64, W)), half_of((256, W)), half_of((256, HD)),
            half_of((256, HD)), whole(PACK),
        ],
        [
            pltpu.VMEM((2, 4, HD, KB), BF), pltpu.VMEM((12, RB, HD), BF),
            pltpu.VMEM((12, RB, HD), BF), pltpu.VMEM((2, 2, 256, HD), BF),
            pltpu.VMEM((2, HD, 256), BF), pltpu.VMEM((2, 4, KB, HD), F4),
            pltpu.VMEM((2, 4, KB, HD), F4), pltpu.VMEM((12, HD, RB), F4),
            pltpu.VMEM((2, 256, HD), F4), pltpu.VMEM((2, 256, HD), F4),
        ],
        flops=4 * 10**10,
    )


def pick_kv_kernel(info, k, v, out):
    out[0] = k[...]
    out[1] = v[...]


def pick_kv(info, prompt_k, prompt_v):
    return call(
        pick_kv_kernel, info, (prompt_k, prompt_v), [half_of((2, 64, HD), 1)] * 2,
        [((2, 2, 64, HD), BF)], [whole((2, 2, 64, HD))],
    )[0]


def spread_kv_kernel(info, k, v, other, out):
    own = info[0]
    mine = jnp.stack([k[...], v[...]])
    theirs = other[...]
    for dest in range(out.shape[0]):
        out[dest, own] = mine
        out[dest, 1 - own] = theirs


def spread_kv(info, prompt_k, prompt_v, other, ring):
    shape = (ring, 2, 2, 2, 64, HD)
    return call(
        spread_kv_kernel, info, (prompt_k, prompt_v, other),
        [half_of((2, 64, HD))] * 2 + [whole((2, 2, 64, HD))],
        [(shape, BF)], [whole(shape)],
    )[0]


def pick_rows_kernel(info, qp, qs, ks, vs, out):
    out[:128] = qp[...].reshape(128, W)
    out[128:384] = qs[...]
    for n in range(4):
        out[384:448, cols(n)] = ks[n * 64 : n * 64 + 64, :]
        out[384:448, cols(4 + n)] = vs[n * 64 : n * 64 + 64, :]


def pick_rows(info, prompt_q, resp_q, resp_k, resp_v):
    return call(
        pick_rows_kernel, info, (prompt_q, resp_q, resp_k, resp_v),
        [half_of((2, 64, W), 1), half_of((256, W), 1), half_of((256, HD), 1), half_of((256, HD), 1)],
        [(PACK, BF)], [whole(PACK)],
    )[0]


def column(i):
    return 2 * (i % 4) + i // 4


def split_cot_kernel(info, dp, dr, out):
    out[0, :32] = dp[...].reshape(32, W)
    out[0, 32:] = dr[...]


def split_cot(info, d_prompt, d_resp):
    return call(
        split_cot_kernel, info, (d_prompt, d_resp),
        [
            pl.BlockSpec((2, 16, W), lambda i, info: (0, 0, column(i))),
            pl.BlockSpec((64, W), lambda i, info: (0, column(i))),
        ],
        [((8, 96, W), BF)], [pl.BlockSpec((1, 96, W), lambda i, info: (i, 0, 0))], grid=(8,),
    )[0]


def place_out_kernel(info, piece, prompt_out, resp_out):
    prompt_out[...] = piece[0, :32].astype(F4).reshape(2, 16, W)
    resp_out[...] = piece[0, 32:].astype(F4)


def place_out(info, pieces):
    return call(
        place_out_kernel, info, (pieces,),
        [pl.BlockSpec((1, 96, W), lambda i, info: (i, 0, 0))],
        [((2, 16, 8 * W), F4), ((64, 8 * W), F4)],
        [
            pl.BlockSpec((2, 16, W), lambda i, info: (0, 0, column(i))),
            pl.BlockSpec((64, W), lambda i, info: (0, column(i))),
        ],
        grid=(8,),
    )


def place_rows_kernel(info, pack, *refs):
    dqp, dqs, drk, drv = refs[4:]
    dqp[...] = pack[:128].astype(F4).reshape(2, 64, W)
    dqs[...] = pack[128:384].astype(F4)
    for n in range(4):
        drk[n * 64 : n * 64 + 64, :] = pack[384:448, cols(n)].astype(F4)
        drv[n * 64 : n * 64 + 64, :] = pack[384:448, cols(4 + n)].astype(F4)


def place_rows(info, pack, parts):
    return call(
        place_rows_kernel, info, (pack, *parts), [whole(PACK)] + [ANY] * 4,
        [(part.shape, F4) for part in parts],
        [half_of((2, 64, W), 1), half_of((256, W), 1), half_of((256, HD), 1), half_of((256, HD), 1)],
        aliases={2: 0, 3: 1, 4: 2, 5: 3},
    )


def sum_terms_kernel(info, terms, own, send):
    for half, ref in ((info[0], own), (1 - info[0], send)):
        total = terms[0, half].astype(F4)
        for source in range(1, terms.shape[0]):
            total = total + terms[source, half].astype(F4)
        ref[...] = total


def sum_terms(info, terms):
    shape = (2, 2, 64, HD)
    return call(
        sum_terms_kernel, info, (terms,), [whole(terms.shape)],
        [(shape, F4)] * 2, [whole(shape)] * 2,
    )


def place_kv_kernel(info, own, other, dk, dv):
    start = pl.multiple_of(info[0] * HD, HD)
    rest = pl.multiple_of((1 - info[0]) * HD, HD)
    for which, ref in ((0, dk), (1, dv)):
        ref[:, :, pl.ds(start, HD)] = own[which]
        ref[:, :, pl.ds(rest, HD)] = other[which]


def place_kv(info, own, other):
    shape = (2, 64, 2 * HD)
    return call(
        place_kv_kernel, info, (own, other), [whole(own.shape)] * 2,
        [(shape, F4)] * 2, [whole(shape)] * 2,
    )


def slot_state(slot_resp, resp_len, resp_prompt):
    same = (slot_resp[0] == slot_resp[1]).astype(jnp.int32)
    block = jnp.stack([jnp.zeros((), jnp.int32), same])
    live = ((slot_resp < 1) & (block < resp_len[0])).astype(jnp.int32)
    seq = lax.axis_index(("half", "ring")).astype(jnp.int32)
    return jnp.stack([seq, live[0], live[1], resp_prompt[0]])


def exchange(array, axis):
    return lax.all_to_all(array, axis, split_axis=0, concat_axis=0, tiled=True)


def swap(array):
    return lax.ppermute(array, "half", [(0, 1), (1, 0)])


def after(array, earlier):
    return lax.optimization_barrier((array, earlier))[0]


def shards(
    prompt_q, prompt_k, prompt_v, resp_q, resp_k, resp_v, slot_resp, resp_len, resp_prompt,
    d_prompt_out, d_resp_out,
):
    ring = lax.axis_size("ring")
    half = lax.axis_index("half").astype(jnp.int32).reshape(1)
    kv_other = swap(pick_kv(half, prompt_k, prompt_v))
    kv = exchange(spread_kv(half, prompt_k, prompt_v, kv_other, ring), "ring")
    state = slot_state(slot_resp, resp_len, resp_prompt)
    rows_other = swap(pick_rows(half, prompt_q, resp_q, resp_k, resp_v))
    info = jnp.concatenate([half, state, swap(state)])
    rows = (resp_k, resp_v, prompt_q, resp_q, rows_other)
    cot = exchange(after(split_cot(half, d_prompt_out, d_resp_out), kv), ("half", "head"))
    pieces, out_t, lse = fwd(info, kv, rows)
    pieces = exchange(pieces, ("half", "head"))
    table, *own_rows, pack = bwd(info, kv, rows, cot, out_t, lse)
    table, pieces = lax.optimization_barrier((table, pieces))
    terms = exchange(table, "ring")
    done = (*place_out(half, pieces), *place_rows(half, swap(pack), own_rows))
    terms, done = lax.optimization_barrier((terms, done))
    prompt_out, resp_out, d_prompt_q, d_resp_q, d_resp_k, d_resp_v = done
    own_kv, send_kv = sum_terms(half, terms)
    d_prompt_k, d_prompt_v = place_kv(half, own_kv, swap(send_kv))
    return (
        prompt_out, resp_out, d_prompt_q, d_prompt_k, d_prompt_v, d_resp_q, d_resp_k, d_resp_v,
    )


def solution(mesh):
    n_seq, n_head = mesh.devices.shape
    fine = Mesh(mesh.devices.reshape(2, n_seq // 2, n_head), ("half", "ring", "head"))
    seq = ("half", "ring")
    grid_rows = (*seq, "head")
    placed = (
        P(None, seq, "head"), P(None, seq, "head"), P(None, seq, "head"),
        P(seq, "head"), P(seq, "head"), P(seq, "head"),
        P(seq), P(seq), P(seq),
        P(None, grid_rows, None), P(grid_rows, None),
    )
    return jax.shard_map(
        shards,
        mesh=fine,
        in_specs=placed,
        out_specs=(
            P(None, grid_rows, None), P(grid_rows, None),
            P(None, seq, "head"), P(None, seq, "head"), P(None, seq, "head"),
            P(seq, "head"), P(seq, "head"), P(seq, "head"),
        ),
        check_vma=False,
    )
```

```python
import jax
import jax.numpy as jnp
from jax import lax
from jax.experimental import pallas as pl
from jax.experimental.pallas import tpu as pltpu
from jax.sharding import Mesh
from jax.sharding import PartitionSpec as P

BF = jnp.bfloat16
F4 = jnp.float32
HD = 128
G = 8
W = G * HD
KB = 512
RB = 512
NEG = -1e30
LIMIT = 55.0
SCALE = HD**-0.5
PARAMS = pltpu.CompilerParams(vmem_limit_bytes=56 * 2**20)
SEQ, LIVE, PROMPT, SOURCE = 1, 2, 4, 4


def nt(a, b):
    return lax.dot_general(a, b, (((1,), (1,)), ((), ())), preferred_element_type=F4)


def nn(a, b):
    return lax.dot_general(a, b, (((1,), (0,)), ((), ())), preferred_element_type=F4)


def cols(g):
    return slice(g * HD, (g + 1) * HD)


def kv_block(kv, which, p, j):
    ring = pl.multiple_of((j & 1) * 8, 8)
    return kv[pl.ds(ring, 8), j >> 1, which, p].reshape(KB, HD)


def causal_mask(seq, j):
    key = j * KB + lax.broadcasted_iota(jnp.int32, (KB, RB), 0)
    row = seq * 64 + (lax.broadcasted_iota(jnp.int32, (KB, RB), 1) & 63)
    return key <= row


def self_mask(j, live_0):
    key = lax.broadcasted_iota(jnp.int32, (256, RB), 0)
    row = j * 128 + (lax.broadcasted_iota(jnp.int32, (256, RB), 1) & 127)
    first = jnp.where(live_0 > 0, 0, j * 128)
    return (key >= first) & (key <= row)


def load_queries(qx, qp, qs, qr):
    for g in range(G):
        for p in range(2):
            at = pl.ds(g * 64, 64)
            qx[p, at, :] = qp[p, :, cols(g)]
            qx[6 + p, at, :] = qr[p * 64 : p * 64 + 64, cols(g)]
        for j in range(2):
            at = pl.ds((g % 4) * 128, 128)
            qx[2 + 2 * j + g // 4, at, :] = qs[j * 128 : j * 128 + 128, cols(g)]
            qx[8 + 2 * j + g // 4, at, :] = qr[128 + j * 128 : 256 + j * 128, cols(g)]


def load_own_pairs(kx, ks, vs, qr):
    for which, ref in ((0, ks), (1, vs)):
        kx[0, which] = ref[...]
        for n in range(4):
            kx[1, which, n * 64 : n * 64 + 64, :] = qr[384:448, cols(which * 4 + n)]


def step(k, q, vt, m, l, acc, mask=None):
    s = nt(k, q)
    if mask is not None:
        s = jnp.where(mask, s, NEG)
    top = jnp.maximum(m, jnp.max(s, 0, keepdims=True))
    p = jnp.exp((s - top) * SCALE)
    fade = jnp.exp((m - top) * SCALE)
    l = l * fade + jnp.sum(p, 0, keepdims=True)
    return top, l, acc * fade + nn(vt, p.astype(BF))


def small_step(k, q, vt, m, l, acc, mask=None):
    p = jnp.exp(nt(k, q) * SCALE)
    if mask is not None:
        p = jnp.where(mask, p, 0.0)
    return m, l + jnp.sum(p, 0, keepdims=True), acc + nn(vt, p.astype(BF))


def top_norm(blocks):
    ones = jnp.ones((8, HD), BF)
    top = jnp.zeros((8, 1), F4)
    for block in blocks:
        top = jnp.maximum(top, jnp.max(nt(ones, block * block), 1, keepdims=True))
    return jnp.max(top)


def fwd_kernel(info, kv, ks, vs, qp, qs, qr, o, ot, lse, vt, qx, kx, vst):
    load_queries(qx, qp, qs, qr)
    load_own_pairs(kx, ks, vs, qr)
    keys = [kv_block(kv, 0, p, j) for p in range(2) for j in range(4)] + [kx[0, 0], kx[1, 0]]
    limit = top_norm([qx[n] for n in range(12)]) * top_norm(keys) * (1.05 * SCALE * SCALE)
    args = (info, kv, qx, kx, o, ot, lse, vt, vst)

    @pl.when(limit < LIMIT * LIMIT)
    def _():
        fwd_rows(small_step, 0.0, *args)

    @pl.when(jnp.logical_not(limit < LIMIT * LIMIT))
    def _():
        fwd_rows(step, NEG, *args)


def fwd_rows(step, start, info, kv, qx, kx, o, ot, lse, vt, vst):
    for p in range(2):
        for j in range(4):
            vt[p, j] = kv_block(kv, 1, p, j).T
    for b in range(2):
        vst[b] = kx[b, 1].T
    m0 = jnp.full((1, RB), start, F4)
    l0 = jnp.zeros((1, RB), F4)

    def finish(at, m, l, acc):
        acc = acc * (1.0 / l)
        ot[at] = acc
        lse[at] = m * SCALE + jnp.log(l)
        return acc.T.astype(BF)

    def prompts(b, carry):
        seq = info[SEQ + SOURCE * b]
        group = (info[0] ^ b) * 4
        last = seq >> 3
        for p in range(2):
            ot[6 * b + p] = jnp.zeros((HD, RB), F4)

        def body(j, c, masked=False):
            mask = causal_mask(seq, j) if masked else None
            out = []
            for p in range(2):
                m, l, acc = step(
                    kv_block(kv, 0, p, j), qx[6 * b + p], vt[p, j],
                    c[2 * p], c[2 * p + 1], ot[6 * b + p], mask,
                )
                ot[6 * b + p] = acc
                out += [m, l]
            return tuple(out)

        c = lax.fori_loop(0, last, body, (m0, l0, m0, l0))
        c = body(last, c, True)
        for p in range(2):
            rows = finish(6 * b + p, c[2 * p], c[2 * p + 1], ot[6 * b + p])
            for g in range(G):
                o[pl.ds(group, 4), p * 16 : p * 16 + 16, cols(g)] = rows[
                    g * 64 : g * 64 + 64
                ].reshape(4, 16, HD)
        return carry

    lax.fori_loop(0, 2, prompts, 0)

    def slots(n, carry):
        b, j = n >> 1, n & 1
        live = info[SEQ + SOURCE * b + 1 + j]
        live_0 = info[SEQ + SOURCE * b + 1]
        prompt = info[SEQ + SOURCE * b + 3]
        group = (info[0] ^ b) * 4 + 2 * j
        at = 6 * b + 2 + 2 * j

        @pl.when(live > 0)
        def _():
            state = [(m0, l0, jnp.zeros((HD, RB), F4))] * 2
            for kb in range(4):
                for h in range(2):
                    state[h] = step(
                        kv_block(kv, 0, prompt, kb), qx[at + h], vt[prompt, kb], *state[h]
                    )
            mask = self_mask(j, live_0)
            for h in range(2):
                rows = finish(at + h, *step(kx[b, 0], qx[at + h], vst[b], *state[h], mask=mask))
                for g in range(4):
                    o[pl.ds(group, 2), 32:96, cols(4 * h + g)] = rows[
                        g * 128 : g * 128 + 128
                    ].reshape(2, 64, HD)

        @pl.when(live == 0)
        def _():
            o[pl.ds(group, 2), 32:96, :] = jnp.zeros((2, 64, W), BF)

        return carry

    lax.fori_loop(0, 4, slots, 0)


def grads(k, v, q, do, kt, total, delta, mask=None):
    s = nt(k, q)
    dp = nt(v, do)
    e = s * SCALE - total
    if mask is not None:
        e = jnp.where(mask, e, NEG)
    p = jnp.exp(e)
    ds = (p * (dp - delta)).astype(BF)
    return nn(p.astype(BF), do), nn(ds, q), nn(kt, ds)


def bwd_kernel(
    info, kv, ks, vs, qp, qs, qr, do, ot, lse,
    tab, dqp, dqs, drk, drv, send, kt, qx, dx, kx, kst, dk, dv, dqt, dkx, dvx,
):
    load_queries(qx, qp, qs, qr)
    load_own_pairs(kx, ks, vs, qr)
    for b in range(2):
        group = (info[0] ^ b) * 4
        for g in range(G):
            for p in range(2):
                dx[6 * b + p, g * 64 : g * 64 + 64, :] = do[
                    pl.ds(group, 4), p * 16 : p * 16 + 16, cols(g)
                ].reshape(64, HD)
            for j in range(2):
                dx[6 * b + 2 + 2 * j + g // 4, (g % 4) * 128 : (g % 4) * 128 + 128, :] = do[
                    pl.ds(group + 2 * j, 2), 32:96, cols(g)
                ].reshape(128, HD)
        kst[b] = kx[b, 0].T
    for p in range(2):
        for j in range(4):
            kt[p, j] = kv_block(kv, 0, p, j).T
    for ref in (dk, dv, dkx, dvx):
        ref[...] = jnp.zeros_like(ref)

    def row_delta(at):
        return jnp.sum(dx[at].astype(F4).T * ot[at], 0, keepdims=True)

    def prompts(b, carry):
        seq = info[SEQ + SOURCE * b]
        last = seq >> 3
        delta = [row_delta(6 * b + p) for p in range(2)]
        for p in range(2):
            dqt[6 * b + p] = jnp.zeros((HD, RB), F4)

        def body(j, c, masked=False):
            mask = causal_mask(seq, j) if masked else None
            for p in range(2):
                at = 6 * b + p
                a_v, a_k, a_q = grads(
                    kv_block(kv, 0, p, j), kv_block(kv, 1, p, j), qx[at], dx[at], kt[p, j],
                    lse[at], delta[p], mask,
                )
                dv[p, j] += a_v
                dk[p, j] += a_k
                dqt[at] += a_q
            return c

        lax.fori_loop(0, last, body, 0)
        body(last, 0, True)
        return carry

    lax.fori_loop(0, 2, prompts, 0)

    def slots(n, carry):
        b, j = n >> 1, n & 1
        live = info[SEQ + SOURCE * b + 1 + j]
        live_0 = info[SEQ + SOURCE * b + 1]
        prompt = info[SEQ + SOURCE * b + 3]

        @pl.when(live > 0)
        def _():
            mask = self_mask(j, live_0)
            for h in range(2):
                at = 6 * b + 2 + 2 * j + h
                q, d, total = qx[at], dx[at], lse[at]
                delta = row_delta(at)
                acc = jnp.zeros((HD, RB), F4)
                for kb in range(4):
                    a_v, a_k, a_q = grads(
                        kv_block(kv, 0, prompt, kb), kv_block(kv, 1, prompt, kb), q, d,
                        kt[prompt, kb], total, delta,
                    )
                    dv[prompt, kb] += a_v
                    dk[prompt, kb] += a_k
                    acc = acc + a_q
                a_v, a_k, a_q = grads(kx[b, 0], kx[b, 1], q, d, kst[b], total, delta, mask)
                dvx[b] += a_v
                dkx[b] += a_k
                dqt[at] = acc + a_q

        @pl.when(live == 0)
        def _():
            for h in range(2):
                dqt[6 * b + 2 + 2 * j + h] = jnp.zeros((HD, RB), F4)

        return carry

    lax.fori_loop(0, 4, slots, 0)
    for b in range(2):
        for p in range(2):
            rows = (dqt[6 * b + p] * SCALE).T
            for g in range(G):
                part = rows[g * 64 : g * 64 + 64]
                if b == 0:
                    dqp[p, :, cols(g)] = part
                else:
                    send[p * 64 : p * 64 + 64, cols(g)] = part.astype(BF)
        for n in range(4):
            rows = (dqt[6 * b + 2 + n] * SCALE).T
            j, h = n // 2, n % 2
            for g in range(4):
                part = rows[g * 128 : g * 128 + 128]
                if b == 0:
                    dqs[j * 128 : j * 128 + 128, cols(4 * h + g)] = part
                else:
                    send[128 + j * 128 : 256 + j * 128, cols(4 * h + g)] = part.astype(BF)
    drk[...] = dkx[0] * SCALE
    drv[...] = dvx[0]
    for n in range(4):
        send[384:448, cols(n)] = (dkx[1, n * 64 : n * 64 + 64, :] * SCALE).astype(BF)
        send[384:448, cols(4 + n)] = dvx[1, n * 64 : n * 64 + 64, :].astype(BF)
    for p in range(2):
        for j in range(4):
            ring = (j & 1) * 8
            tab[ring : ring + 8, j >> 1, 0, p] = (dk[p, j] * SCALE).astype(BF).reshape(8, 64, HD)
            tab[ring : ring + 8, j >> 1, 1, p] = dv[p, j].astype(BF).reshape(8, 64, HD)


def whole(shape):
    return pl.BlockSpec(tuple(shape), lambda i, info: (0,) * len(shape))


def half_of(shape, other=0):
    lead = (0,) * (len(shape) - 1)
    return pl.BlockSpec(tuple(shape), lambda i, info: lead + (info[0] ^ other,))


ANY = pl.BlockSpec(memory_space=pl.ANY)


def call(kernel, info, ins, in_specs, outs, out_specs, scratch=(), grid=(1,), flops=0, aliases=None):
    name = kernel.__name__.replace("_kernel", "")
    return pl.pallas_call(
        kernel,
        grid_spec=pltpu.PrefetchScalarGridSpec(
            num_scalar_prefetch=1, grid=grid, in_specs=in_specs, out_specs=out_specs,
            scratch_shapes=list(scratch),
        ),
        out_shape=[jax.ShapeDtypeStruct(shape, dtype) for shape, dtype in outs],
        input_output_aliases=aliases or {},
        cost_estimate=pl.CostEstimate(
            flops=flops, bytes_accessed=4 * 10**6, transcendentals=flops // 1000
        ),
        compiler_params=PARAMS,
        name=name,
    )(info, *ins)


PACK = (384 + 64, W)
ROWS = [half_of((256, HD)), half_of((256, HD)), half_of((2, 64, W)), half_of((256, W)), whole(PACK)]
STATE = [((12, HD, RB), F4), ((12, 1, RB), F4)]


def fwd(info, kv, rows):
    return call(
        fwd_kernel, info, (kv, *rows), [whole(kv.shape), *ROWS],
        [((8, 96, W), BF), *STATE],
        [whole((8, 96, W)), *(whole(shape) for shape, _ in STATE)],
        [
            pltpu.VMEM((2, 4, HD, KB), BF), pltpu.VMEM((12, RB, HD), BF),
            pltpu.VMEM((2, 2, 256, HD), BF), pltpu.VMEM((2, HD, 256), BF),
        ],
        flops=2 * 10**10,
    )


def bwd(info, kv, rows, cot, out_t, lse):
    return call(
        bwd_kernel, info, (kv, *rows, cot, out_t, lse),
        [whole(kv.shape), *ROWS, whole(cot.shape), *(whole(shape) for shape, _ in STATE)],
        [
            (kv.shape, BF), ((2, 64, 2 * W), F4), ((256, 2 * W), F4),
            ((256, 2 * HD), F4), ((256, 2 * HD), F4), (PACK, BF),
        ],
        [
            whole(kv.shape), half_of((2, 64, W)), half_of((256, W)), half_of((256, HD)),
            half_of((256, HD)), whole(PACK),
        ],
        [
            pltpu.VMEM((2, 4, HD, KB), BF), pltpu.VMEM((12, RB, HD), BF),
            pltpu.VMEM((12, RB, HD), BF), pltpu.VMEM((2, 2, 256, HD), BF),
            pltpu.VMEM((2, HD, 256), BF), pltpu.VMEM((2, 4, KB, HD), F4),
            pltpu.VMEM((2, 4, KB, HD), F4), pltpu.VMEM((12, HD, RB), F4),
            pltpu.VMEM((2, 256, HD), F4), pltpu.VMEM((2, 256, HD), F4),
        ],
        flops=4 * 10**10,
    )


def pick_kv_kernel(info, k, v, out):
    out[0] = k[...]
    out[1] = v[...]


def pick_kv(info, prompt_k, prompt_v):
    return call(
        pick_kv_kernel, info, (prompt_k, prompt_v), [half_of((2, 64, HD), 1)] * 2,
        [((2, 2, 64, HD), BF)], [whole((2, 2, 64, HD))],
    )[0]


def spread_kv_kernel(info, k, v, other, out):
    own = info[0]
    mine = jnp.stack([k[...], v[...]])
    theirs = other[...]
    for dest in range(out.shape[0]):
        out[dest, own] = mine
        out[dest, 1 - own] = theirs


def spread_kv(info, prompt_k, prompt_v, other, ring):
    shape = (ring, 2, 2, 2, 64, HD)
    return call(
        spread_kv_kernel, info, (prompt_k, prompt_v, other),
        [half_of((2, 64, HD))] * 2 + [whole((2, 2, 64, HD))],
        [(shape, BF)], [whole(shape)],
    )[0]


def pick_rows_kernel(info, qp, qs, ks, vs, out):
    out[:128] = qp[...].reshape(128, W)
    out[128:384] = qs[...]
    for n in range(4):
        out[384:448, cols(n)] = ks[n * 64 : n * 64 + 64, :]
        out[384:448, cols(4 + n)] = vs[n * 64 : n * 64 + 64, :]


def pick_rows(info, prompt_q, resp_q, resp_k, resp_v):
    return call(
        pick_rows_kernel, info, (prompt_q, resp_q, resp_k, resp_v),
        [half_of((2, 64, W), 1), half_of((256, W), 1), half_of((256, HD), 1), half_of((256, HD), 1)],
        [(PACK, BF)], [whole(PACK)],
    )[0]


def column(i):
    return 2 * (i % 4) + i // 4


def split_cot_kernel(info, dp, dr, out):
    out[0, :32] = dp[...].reshape(32, W)
    out[0, 32:] = dr[...]


def split_cot(info, d_prompt, d_resp):
    return call(
        split_cot_kernel, info, (d_prompt, d_resp),
        [
            pl.BlockSpec((2, 16, W), lambda i, info: (0, 0, column(i))),
            pl.BlockSpec((64, W), lambda i, info: (0, column(i))),
        ],
        [((8, 96, W), BF)], [pl.BlockSpec((1, 96, W), lambda i, info: (i, 0, 0))], grid=(8,),
    )[0]


def place_out_kernel(info, piece, prompt_out, resp_out):
    prompt_out[...] = piece[0, :32].astype(F4).reshape(2, 16, W)
    resp_out[...] = piece[0, 32:].astype(F4)


def place_out(info, pieces):
    return call(
        place_out_kernel, info, (pieces,),
        [pl.BlockSpec((1, 96, W), lambda i, info: (i, 0, 0))],
        [((2, 16, 8 * W), F4), ((64, 8 * W), F4)],
        [
            pl.BlockSpec((2, 16, W), lambda i, info: (0, 0, column(i))),
            pl.BlockSpec((64, W), lambda i, info: (0, column(i))),
        ],
        grid=(8,),
    )


def place_rows_kernel(info, pack, *refs):
    dqp, dqs, drk, drv = refs[4:]
    dqp[...] = pack[:128].astype(F4).reshape(2, 64, W)
    dqs[...] = pack[128:384].astype(F4)
    for n in range(4):
        drk[n * 64 : n * 64 + 64, :] = pack[384:448, cols(n)].astype(F4)
        drv[n * 64 : n * 64 + 64, :] = pack[384:448, cols(4 + n)].astype(F4)


def place_rows(info, pack, parts):
    return call(
        place_rows_kernel, info, (pack, *parts), [whole(PACK)] + [ANY] * 4,
        [(part.shape, F4) for part in parts],
        [half_of((2, 64, W), 1), half_of((256, W), 1), half_of((256, HD), 1), half_of((256, HD), 1)],
        aliases={2: 0, 3: 1, 4: 2, 5: 3},
    )


def sum_terms_kernel(info, terms, own, send):
    for half, ref in ((info[0], own), (1 - info[0], send)):
        total = terms[0, half].astype(F4)
        for source in range(1, terms.shape[0]):
            total = total + terms[source, half].astype(F4)
        ref[...] = total


def sum_terms(info, terms):
    shape = (2, 2, 64, HD)
    return call(
        sum_terms_kernel, info, (terms,), [whole(terms.shape)],
        [(shape, F4)] * 2, [whole(shape)] * 2,
    )


def place_kv_kernel(info, own, other, dk, dv):
    start = pl.multiple_of(info[0] * HD, HD)
    rest = pl.multiple_of((1 - info[0]) * HD, HD)
    for which, ref in ((0, dk), (1, dv)):
        ref[:, :, pl.ds(start, HD)] = own[which]
        ref[:, :, pl.ds(rest, HD)] = other[which]


def place_kv(info, own, other):
    shape = (2, 64, 2 * HD)
    return call(
        place_kv_kernel, info, (own, other), [whole(own.shape)] * 2,
        [(shape, F4)] * 2, [whole(shape)] * 2,
    )


def slot_state(slot_resp, resp_len, resp_prompt):
    same = (slot_resp[0] == slot_resp[1]).astype(jnp.int32)
    block = jnp.stack([jnp.zeros((), jnp.int32), same])
    live = ((slot_resp < 1) & (block < resp_len[0])).astype(jnp.int32)
    seq = lax.axis_index(("half", "ring")).astype(jnp.int32)
    return jnp.stack([seq, live[0], live[1], resp_prompt[0]])


def exchange(array, axis):
    return lax.all_to_all(array, axis, split_axis=0, concat_axis=0, tiled=True)


def swap(array):
    return lax.ppermute(array, "half", [(0, 1), (1, 0)])


def after(array, earlier):
    return lax.optimization_barrier((array, earlier))[0]


def shards(
    prompt_q, prompt_k, prompt_v, resp_q, resp_k, resp_v, slot_resp, resp_len, resp_prompt,
    d_prompt_out, d_resp_out,
):
    ring = lax.axis_size("ring")
    half = lax.axis_index("half").astype(jnp.int32).reshape(1)
    kv_other = swap(pick_kv(half, prompt_k, prompt_v))
    kv = exchange(spread_kv(half, prompt_k, prompt_v, kv_other, ring), "ring")
    state = slot_state(slot_resp, resp_len, resp_prompt)
    state_other = swap(state)
    rows_out, state_other = lax.optimization_barrier(
        (pick_rows(half, prompt_q, resp_q, resp_k, resp_v), state_other)
    )
    rows_other = swap(rows_out)
    info = jnp.concatenate([half, state, state_other])
    rows = (resp_k, resp_v, prompt_q, resp_q, rows_other)
    cot = exchange(after(split_cot(half, d_prompt_out, d_resp_out), kv), ("half", "head"))
    pieces, out_t, lse = fwd(info, kv, rows)
    pieces = exchange(pieces, ("half", "head"))
    table, *own_rows, pack = bwd(info, kv, rows, cot, out_t, lse)
    table, pieces = lax.optimization_barrier((table, pieces))
    terms = exchange(table, "ring")
    pack, outs = lax.optimization_barrier((swap(pack), place_out(half, pieces)))
    done = (*outs, *place_rows(half, pack, own_rows))
    terms, done = lax.optimization_barrier((terms, done))
    prompt_out, resp_out, d_prompt_q, d_resp_q, d_resp_k, d_resp_v = done
    own_kv, send_kv = sum_terms(half, terms)
    d_prompt_k, d_prompt_v = place_kv(half, own_kv, swap(send_kv))
    return (
        prompt_out, resp_out, d_prompt_q, d_prompt_k, d_prompt_v, d_resp_q, d_resp_k, d_resp_v,
    )


def solution(mesh):
    n_seq, n_head = mesh.devices.shape
    fine = Mesh(mesh.devices.reshape(2, n_seq // 2, n_head), ("half", "ring", "head"))
    seq = ("half", "ring")
    grid_rows = (*seq, "head")
    placed = (
        P(None, seq, "head"), P(None, seq, "head"), P(None, seq, "head"),
        P(seq, "head"), P(seq, "head"), P(seq, "head"),
        P(seq), P(seq), P(seq),
        P(None, grid_rows, None), P(grid_rows, None),
    )
    return jax.shard_map(
        shards,
        mesh=fine,
        in_specs=placed,
        out_specs=(
            P(None, grid_rows, None), P(grid_rows, None),
            P(None, seq, "head"), P(None, seq, "head"), P(None, seq, "head"),
            P(seq, "head"), P(seq, "head"), P(seq, "head"),
        ),
        check_vma=False,
    )
```

```python
import jax
import jax.numpy as jnp
from jax import lax
from jax.experimental import pallas as pl
from jax.experimental.pallas import tpu as pltpu
from jax.sharding import Mesh
from jax.sharding import PartitionSpec as P

BF = jnp.bfloat16
F4 = jnp.float32
HD = 128
G = 8
W = G * HD
KB = 512
RB = 512
NEG = -1e30
LIMIT = 55.0
SCALE = HD**-0.5
PARAMS = pltpu.CompilerParams(vmem_limit_bytes=56 * 2**20)
SEQ, LIVE, PROMPT, SOURCE = 1, 2, 4, 4


def nt(a, b):
    return lax.dot_general(a, b, (((1,), (1,)), ((), ())), preferred_element_type=F4)


def nn(a, b):
    return lax.dot_general(a, b, (((1,), (0,)), ((), ())), preferred_element_type=F4)


def cols(g):
    return slice(g * HD, (g + 1) * HD)


def kv_block(kv, which, p, j):
    ring = pl.multiple_of((j & 1) * 8, 8)
    return kv[pl.ds(ring, 8), j >> 1, which, p].reshape(KB, HD)


def causal_mask(seq, j):
    key = j * KB + lax.broadcasted_iota(jnp.int32, (KB, RB), 0)
    row = seq * 64 + (lax.broadcasted_iota(jnp.int32, (KB, RB), 1) & 63)
    return key <= row


def self_mask(j, live_0):
    key = lax.broadcasted_iota(jnp.int32, (256, RB), 0)
    row = j * 128 + (lax.broadcasted_iota(jnp.int32, (256, RB), 1) & 127)
    first = jnp.where(live_0 > 0, 0, j * 128)
    return (key >= first) & (key <= row)


def load_queries(qx, qp, qs, qr):
    for g in range(G):
        for p in range(2):
            at = pl.ds(g * 64, 64)
            qx[p, at, :] = qp[p, :, cols(g)]
            qx[6 + p, at, :] = qr[p * 64 : p * 64 + 64, cols(g)]
        for j in range(2):
            at = pl.ds((g % 4) * 128, 128)
            qx[2 + 2 * j + g // 4, at, :] = qs[j * 128 : j * 128 + 128, cols(g)]
            qx[8 + 2 * j + g // 4, at, :] = qr[128 + j * 128 : 256 + j * 128, cols(g)]


def load_own_pairs(kx, ks, vs, qr):
    for which, ref in ((0, ks), (1, vs)):
        kx[0, which] = ref[...]
        for n in range(4):
            kx[1, which, n * 64 : n * 64 + 64, :] = qr[384:448, cols(which * 4 + n)]


def step(k, q, vt, m, l, acc, mask=None):
    s = nt(k, q)
    if mask is not None:
        s = jnp.where(mask, s, NEG)
    top = jnp.maximum(m, jnp.max(s, 0, keepdims=True))
    p = jnp.exp((s - top) * SCALE)
    fade = jnp.exp((m - top) * SCALE)
    l = l * fade + jnp.sum(p, 0, keepdims=True)
    return top, l, acc * fade + nn(vt, p.astype(BF))


def small_step(k, q, vt, m, l, acc, mask=None):
    p = jnp.exp(nt(k, q) * SCALE)
    if mask is not None:
        p = jnp.where(mask, p, 0.0)
    return m, l + jnp.sum(p, 0, keepdims=True), acc + nn(vt, p.astype(BF))


def top_norm(blocks):
    ones = jnp.ones((8, HD), BF)
    top = jnp.zeros((8, 1), F4)
    for block in blocks:
        top = jnp.maximum(top, jnp.max(nt(ones, block * block), 1, keepdims=True))
    return jnp.max(top)


def fwd_kernel(info, kv, ks, vs, qp, qs, qr, o, lse, ot, vt, qx, kx, vst):
    load_queries(qx, qp, qs, qr)
    load_own_pairs(kx, ks, vs, qr)
    keys = [kv_block(kv, 0, p, j) for p in range(2) for j in range(4)] + [kx[0, 0], kx[1, 0]]
    limit = top_norm([qx[n] for n in range(12)]) * top_norm(keys) * (1.05 * SCALE * SCALE)
    args = (info, kv, qx, kx, o, ot, lse, vt, vst)

    @pl.when(limit < LIMIT * LIMIT)
    def _():
        fwd_rows(small_step, 0.0, *args)

    @pl.when(jnp.logical_not(limit < LIMIT * LIMIT))
    def _():
        fwd_rows(step, NEG, *args)


def fwd_rows(step, start, info, kv, qx, kx, o, ot, lse, vt, vst):
    for p in range(2):
        for j in range(4):
            vt[p, j] = kv_block(kv, 1, p, j).T
    for b in range(2):
        vst[b] = kx[b, 1].T
    m0 = jnp.full((1, RB), start, F4)
    l0 = jnp.zeros((1, RB), F4)

    def finish(at, m, l, acc):
        acc = acc * (1.0 / l)
        lse[at] = m * SCALE + jnp.log(l)
        return acc.T.astype(BF)

    def prompts(b, carry):
        seq = info[SEQ + SOURCE * b]
        group = (info[0] ^ b) * 4
        last = seq >> 3
        for p in range(2):
            ot[p] = jnp.zeros((HD, RB), F4)

        def body(j, c, masked=False):
            mask = causal_mask(seq, j) if masked else None
            out = []
            for p in range(2):
                m, l, acc = step(
                    kv_block(kv, 0, p, j), qx[6 * b + p], vt[p, j],
                    c[2 * p], c[2 * p + 1], ot[p], mask,
                )
                ot[p] = acc
                out += [m, l]
            return tuple(out)

        c = lax.fori_loop(0, last, body, (m0, l0, m0, l0))
        c = body(last, c, True)
        for p in range(2):
            rows = finish(6 * b + p, c[2 * p], c[2 * p + 1], ot[p])
            for g in range(G):
                o[pl.ds(group, 4), p * 16 : p * 16 + 16, cols(g)] = rows[
                    g * 64 : g * 64 + 64
                ].reshape(4, 16, HD)
        return carry

    lax.fori_loop(0, 2, prompts, 0)

    def slots(n, carry):
        b, j = n >> 1, n & 1
        live = info[SEQ + SOURCE * b + 1 + j]
        live_0 = info[SEQ + SOURCE * b + 1]
        prompt = info[SEQ + SOURCE * b + 3]
        group = (info[0] ^ b) * 4 + 2 * j
        at = 6 * b + 2 + 2 * j

        @pl.when(live > 0)
        def _():
            state = [(m0, l0, jnp.zeros((HD, RB), F4))] * 2
            for kb in range(4):
                for h in range(2):
                    state[h] = step(
                        kv_block(kv, 0, prompt, kb), qx[at + h], vt[prompt, kb], *state[h]
                    )
            mask = self_mask(j, live_0)
            for h in range(2):
                rows = finish(at + h, *step(kx[b, 0], qx[at + h], vst[b], *state[h], mask=mask))
                for g in range(4):
                    o[pl.ds(group, 2), 32:96, cols(4 * h + g)] = rows[
                        g * 128 : g * 128 + 128
                    ].reshape(2, 64, HD)

        @pl.when(live == 0)
        def _():
            o[pl.ds(group, 2), 32:96, :] = jnp.zeros((2, 64, W), BF)

        return carry

    lax.fori_loop(0, 4, slots, 0)


def grads(k, v, q, do, kt, total, delta, mask=None):
    s = nt(k, q)
    dp = nt(v, do)
    e = s * SCALE - total
    if mask is not None:
        e = jnp.where(mask, e, NEG)
    p = jnp.exp(e)
    ds = (p * (dp - delta)).astype(BF)
    return nn(p.astype(BF), do), nn(ds, q), nn(kt, ds)


def bwd_kernel(
    info, kv, ks, vs, qp, qs, qr, do, out, lse,
    tab, dqp, dqs, drk, drv, send, kt, qx, dx, ox, kx, kst, dk, dv, dqt, dkx, dvx,
):
    load_queries(qx, qp, qs, qr)
    load_own_pairs(kx, ks, vs, qr)
    for b in range(2):
        group = (info[0] ^ b) * 4
        for rows, ref in ((dx, do), (ox, out)):
            for g in range(G):
                for p in range(2):
                    rows[6 * b + p, g * 64 : g * 64 + 64, :] = ref[
                        pl.ds(group, 4), p * 16 : p * 16 + 16, cols(g)
                    ].reshape(64, HD)
                for j in range(2):
                    at = (g % 4) * 128
                    rows[6 * b + 2 + 2 * j + g // 4, at : at + 128, :] = ref[
                        pl.ds(group + 2 * j, 2), 32:96, cols(g)
                    ].reshape(128, HD)
        kst[b] = kx[b, 0].T
    for p in range(2):
        for j in range(4):
            kt[p, j] = kv_block(kv, 0, p, j).T
    for ref in (dk, dv, dkx, dvx):
        ref[...] = jnp.zeros_like(ref)

    def row_delta(at):
        return jnp.sum((dx[at].astype(F4) * ox[at].astype(F4)).T, 0, keepdims=True)

    def prompts(b, carry):
        seq = info[SEQ + SOURCE * b]
        last = seq >> 3
        delta = [row_delta(6 * b + p) for p in range(2)]
        for p in range(2):
            dqt[6 * b + p] = jnp.zeros((HD, RB), F4)

        def body(j, c, masked=False):
            mask = causal_mask(seq, j) if masked else None
            for p in range(2):
                at = 6 * b + p
                a_v, a_k, a_q = grads(
                    kv_block(kv, 0, p, j), kv_block(kv, 1, p, j), qx[at], dx[at], kt[p, j],
                    lse[at], delta[p], mask,
                )
                dv[p, j] += a_v
                dk[p, j] += a_k
                dqt[at] += a_q
            return c

        lax.fori_loop(0, last, body, 0)
        body(last, 0, True)
        return carry

    lax.fori_loop(0, 2, prompts, 0)

    def slots(n, carry):
        b, j = n >> 1, n & 1
        live = info[SEQ + SOURCE * b + 1 + j]
        live_0 = info[SEQ + SOURCE * b + 1]
        prompt = info[SEQ + SOURCE * b + 3]

        @pl.when(live > 0)
        def _():
            mask = self_mask(j, live_0)
            for h in range(2):
                at = 6 * b + 2 + 2 * j + h
                q, d, total = qx[at], dx[at], lse[at]
                delta = row_delta(at)
                acc = jnp.zeros((HD, RB), F4)
                for kb in range(4):
                    a_v, a_k, a_q = grads(
                        kv_block(kv, 0, prompt, kb), kv_block(kv, 1, prompt, kb), q, d,
                        kt[prompt, kb], total, delta,
                    )
                    dv[prompt, kb] += a_v
                    dk[prompt, kb] += a_k
                    acc = acc + a_q
                a_v, a_k, a_q = grads(kx[b, 0], kx[b, 1], q, d, kst[b], total, delta, mask)
                dvx[b] += a_v
                dkx[b] += a_k
                dqt[at] = acc + a_q

        @pl.when(live == 0)
        def _():
            for h in range(2):
                dqt[6 * b + 2 + 2 * j + h] = jnp.zeros((HD, RB), F4)

        return carry

    lax.fori_loop(0, 4, slots, 0)
    for b in range(2):
        for p in range(2):
            rows = (dqt[6 * b + p] * SCALE).T
            for g in range(G):
                part = rows[g * 64 : g * 64 + 64]
                if b == 0:
                    dqp[p, :, cols(g)] = part
                else:
                    send[p * 64 : p * 64 + 64, cols(g)] = part.astype(BF)
        for n in range(4):
            rows = (dqt[6 * b + 2 + n] * SCALE).T
            j, h = n // 2, n % 2
            for g in range(4):
                part = rows[g * 128 : g * 128 + 128]
                if b == 0:
                    dqs[j * 128 : j * 128 + 128, cols(4 * h + g)] = part
                else:
                    send[128 + j * 128 : 256 + j * 128, cols(4 * h + g)] = part.astype(BF)
    drk[...] = dkx[0] * SCALE
    drv[...] = dvx[0]
    for n in range(4):
        send[384:448, cols(n)] = (dkx[1, n * 64 : n * 64 + 64, :] * SCALE).astype(BF)
        send[384:448, cols(4 + n)] = dvx[1, n * 64 : n * 64 + 64, :].astype(BF)
    for p in range(2):
        for j in range(4):
            ring = (j & 1) * 8
            tab[ring : ring + 8, j >> 1, 0, p] = (dk[p, j] * SCALE).astype(BF).reshape(8, 64, HD)
            tab[ring : ring + 8, j >> 1, 1, p] = dv[p, j].astype(BF).reshape(8, 64, HD)


def whole(shape):
    return pl.BlockSpec(tuple(shape), lambda i, info: (0,) * len(shape))


def half_of(shape, other=0):
    lead = (0,) * (len(shape) - 1)
    return pl.BlockSpec(tuple(shape), lambda i, info: lead + (info[0] ^ other,))


ANY = pl.BlockSpec(memory_space=pl.ANY)


def call(kernel, info, ins, in_specs, outs, out_specs, scratch=(), grid=(1,), flops=0, aliases=None):
    name = kernel.__name__.replace("_kernel", "")
    return pl.pallas_call(
        kernel,
        grid_spec=pltpu.PrefetchScalarGridSpec(
            num_scalar_prefetch=1, grid=grid, in_specs=in_specs, out_specs=out_specs,
            scratch_shapes=list(scratch),
        ),
        out_shape=[jax.ShapeDtypeStruct(shape, dtype) for shape, dtype in outs],
        input_output_aliases=aliases or {},
        cost_estimate=pl.CostEstimate(
            flops=flops, bytes_accessed=4 * 10**6, transcendentals=flops // 1000
        ),
        compiler_params=PARAMS,
        name=name,
    )(info, *ins)


PACK = (384 + 64, W)
ROWS = [half_of((256, HD)), half_of((256, HD)), half_of((2, 64, W)), half_of((256, W)), whole(PACK)]
LSE = (12, 1, RB)


def fwd(info, kv, rows):
    return call(
        fwd_kernel, info, (kv, *rows), [whole(kv.shape), *ROWS],
        [((8, 96, W), BF), (LSE, F4)],
        [whole((8, 96, W)), whole(LSE)],
        [
            pltpu.VMEM((2, HD, RB), F4), pltpu.VMEM((2, 4, HD, KB), BF), pltpu.VMEM((12, RB, HD), BF),
            pltpu.VMEM((2, 2, 256, HD), BF), pltpu.VMEM((2, HD, 256), BF),
        ],
        flops=2 * 10**10,
    )


def bwd(info, kv, rows, cot, pieces, lse):
    return call(
        bwd_kernel, info, (kv, *rows, cot, pieces, lse),
        [whole(kv.shape), *ROWS, whole(cot.shape), whole(cot.shape), whole(LSE)],
        [
            (kv.shape, BF), ((2, 64, 2 * W), F4), ((256, 2 * W), F4),
            ((256, 2 * HD), F4), ((256, 2 * HD), F4), (PACK, BF),
        ],
        [
            whole(kv.shape), half_of((2, 64, W)), half_of((256, W)), half_of((256, HD)),
            half_of((256, HD)), whole(PACK),
        ],
        [
            pltpu.VMEM((2, 4, HD, KB), BF), pltpu.VMEM((12, RB, HD), BF),
            pltpu.VMEM((12, RB, HD), BF), pltpu.VMEM((12, RB, HD), BF),
            pltpu.VMEM((2, 2, 256, HD), BF), pltpu.VMEM((2, HD, 256), BF),
            pltpu.VMEM((2, 4, KB, HD), F4),
            pltpu.VMEM((2, 4, KB, HD), F4), pltpu.VMEM((12, HD, RB), F4),
            pltpu.VMEM((2, 256, HD), F4), pltpu.VMEM((2, 256, HD), F4),
        ],
        flops=4 * 10**10,
    )


def pick_kv_kernel(info, k, v, out):
    out[0] = k[...]
    out[1] = v[...]


def pick_kv(info, prompt_k, prompt_v):
    return call(
        pick_kv_kernel, info, (prompt_k, prompt_v), [half_of((2, 64, HD), 1)] * 2,
        [((2, 2, 64, HD), BF)], [whole((2, 2, 64, HD))],
    )[0]


def spread_kv_kernel(info, k, v, other, out):
    own = info[0]
    mine = jnp.stack([k[...], v[...]])
    theirs = other[...]
    for dest in range(out.shape[0]):
        out[dest, own] = mine
        out[dest, 1 - own] = theirs


def spread_kv(info, prompt_k, prompt_v, other, ring):
    shape = (ring, 2, 2, 2, 64, HD)
    return call(
        spread_kv_kernel, info, (prompt_k, prompt_v, other),
        [half_of((2, 64, HD))] * 2 + [whole((2, 2, 64, HD))],
        [(shape, BF)], [whole(shape)],
    )[0]


def pick_rows_kernel(info, qp, qs, ks, vs, out):
    out[:128] = qp[...].reshape(128, W)
    out[128:384] = qs[...]
    for n in range(4):
        out[384:448, cols(n)] = ks[n * 64 : n * 64 + 64, :]
        out[384:448, cols(4 + n)] = vs[n * 64 : n * 64 + 64, :]


def pick_rows(info, prompt_q, resp_q, resp_k, resp_v):
    return call(
        pick_rows_kernel, info, (prompt_q, resp_q, resp_k, resp_v),
        [half_of((2, 64, W), 1), half_of((256, W), 1), half_of((256, HD), 1), half_of((256, HD), 1)],
        [(PACK, BF)], [whole(PACK)],
    )[0]


def column(i):
    return 2 * (i % 4) + i // 4


def split_cot_kernel(info, dp, dr, out):
    out[0, :32] = dp[...].reshape(32, W)
    out[0, 32:] = dr[...]


def split_cot(info, d_prompt, d_resp):
    return call(
        split_cot_kernel, info, (d_prompt, d_resp),
        [
            pl.BlockSpec((2, 16, W), lambda i, info: (0, 0, column(i))),
            pl.BlockSpec((64, W), lambda i, info: (0, column(i))),
        ],
        [((8, 96, W), BF)], [pl.BlockSpec((1, 96, W), lambda i, info: (i, 0, 0))], grid=(8,),
    )[0]


def place_out_kernel(info, piece, prompt_out, resp_out):
    prompt_out[...] = piece[0, :32].astype(F4).reshape(2, 16, W)
    resp_out[...] = piece[0, 32:].astype(F4)


def place_out(info, pieces):
    return call(
        place_out_kernel, info, (pieces,),
        [pl.BlockSpec((1, 96, W), lambda i, info: (i, 0, 0))],
        [((2, 16, 8 * W), F4), ((64, 8 * W), F4)],
        [
            pl.BlockSpec((2, 16, W), lambda i, info: (0, 0, column(i))),
            pl.BlockSpec((64, W), lambda i, info: (0, column(i))),
        ],
        grid=(8,),
    )


def place_rows_kernel(info, pack, *refs):
    dqp, dqs, drk, drv = refs[4:]
    dqp[...] = pack[:128].astype(F4).reshape(2, 64, W)
    dqs[...] = pack[128:384].astype(F4)
    for n in range(4):
        drk[n * 64 : n * 64 + 64, :] = pack[384:448, cols(n)].astype(F4)
        drv[n * 64 : n * 64 + 64, :] = pack[384:448, cols(4 + n)].astype(F4)


def place_rows(info, pack, parts):
    return call(
        place_rows_kernel, info, (pack, *parts), [whole(PACK)] + [ANY] * 4,
        [(part.shape, F4) for part in parts],
        [half_of((2, 64, W), 1), half_of((256, W), 1), half_of((256, HD), 1), half_of((256, HD), 1)],
        aliases={2: 0, 3: 1, 4: 2, 5: 3},
    )


def sum_terms_kernel(info, terms, out):
    total = terms[0, 0].astype(F4)
    for source in range(1, terms.shape[0]):
        total = total + terms[source, 0].astype(F4)
    out[...] = total


def sum_terms(info, terms, other):
    shape = (2, 2, 64, HD)
    block = (terms.shape[0], 1, *shape)
    return call(
        sum_terms_kernel, info, (terms,),
        [pl.BlockSpec(block, lambda i, info: (0, info[0] ^ other, 0, 0, 0, 0))],
        [(shape, F4)], [whole(shape)],
    )[0]


def place_kv_kernel(info, own, other, dk, dv):
    start = pl.multiple_of(info[0] * HD, HD)
    rest = pl.multiple_of((1 - info[0]) * HD, HD)
    for which, ref in ((0, dk), (1, dv)):
        ref[:, :, pl.ds(start, HD)] = own[which]
        ref[:, :, pl.ds(rest, HD)] = other[which]


def place_kv(info, own, other):
    shape = (2, 64, 2 * HD)
    return call(
        place_kv_kernel, info, (own, other), [whole(own.shape)] * 2,
        [(shape, F4)] * 2, [whole(shape)] * 2,
    )


def slot_state(slot_resp, resp_len, resp_prompt):
    same = (slot_resp[0] == slot_resp[1]).astype(jnp.int32)
    block = jnp.stack([jnp.zeros((), jnp.int32), same])
    live = ((slot_resp < 1) & (block < resp_len[0])).astype(jnp.int32)
    seq = lax.axis_index(("half", "ring")).astype(jnp.int32)
    return jnp.stack([seq, live[0], live[1], resp_prompt[0]])


def exchange(array, axis):
    return lax.all_to_all(array, axis, split_axis=0, concat_axis=0, tiled=True)


def swap(array):
    return lax.ppermute(array, "half", [(0, 1), (1, 0)])


def after(array, earlier):
    return lax.optimization_barrier((array, earlier))[0]


def shards(
    prompt_q, prompt_k, prompt_v, resp_q, resp_k, resp_v, slot_resp, resp_len, resp_prompt,
    d_prompt_out, d_resp_out,
):
    ring = lax.axis_size("ring")
    half = lax.axis_index("half").astype(jnp.int32).reshape(1)
    kv_other = swap(pick_kv(half, prompt_k, prompt_v))
    kv = exchange(spread_kv(half, prompt_k, prompt_v, kv_other, ring), "ring")
    state = slot_state(slot_resp, resp_len, resp_prompt)
    state_other = swap(state)
    rows_out, state_other = lax.optimization_barrier(
        (pick_rows(half, prompt_q, resp_q, resp_k, resp_v), state_other)
    )
    rows_other = swap(rows_out)
    info = jnp.concatenate([half, state, state_other])
    rows = (resp_k, resp_v, prompt_q, resp_q, rows_other)
    cot = exchange(after(split_cot(half, d_prompt_out, d_resp_out), kv), ("half", "head"))
    pieces, lse = fwd(info, kv, rows)
    table, *own_rows, pack = bwd(info, kv, rows, cot, pieces, lse)
    pieces = exchange(pieces, ("half", "head"))
    table, pieces = lax.optimization_barrier((table, pieces))
    terms = exchange(table, "ring")
    pack, outs = lax.optimization_barrier((swap(pack), place_out(half, pieces)))
    done = (*outs, *place_rows(half, pack, own_rows))
    terms, done = lax.optimization_barrier((terms, done))
    prompt_out, resp_out, d_prompt_q, d_resp_q, d_resp_k, d_resp_v = done
    send_kv = swap(sum_terms(half, terms, 1))
    own_kv = sum_terms(half, terms, 0)
    d_prompt_k, d_prompt_v = place_kv(half, own_kv, send_kv)
    return (
        prompt_out, resp_out, d_prompt_q, d_prompt_k, d_prompt_v, d_resp_q, d_resp_k, d_resp_v,
    )


def solution(mesh):
    n_seq, n_head = mesh.devices.shape
    fine = Mesh(mesh.devices.reshape(2, n_seq // 2, n_head), ("half", "ring", "head"))
    seq = ("half", "ring")
    grid_rows = (*seq, "head")
    placed = (
        P(None, seq, "head"), P(None, seq, "head"), P(None, seq, "head"),
        P(seq, "head"), P(seq, "head"), P(seq, "head"),
        P(seq), P(seq), P(seq),
        P(None, grid_rows, None), P(grid_rows, None),
    )
    return jax.shard_map(
        shards,
        mesh=fine,
        in_specs=placed,
        out_specs=(
            P(None, grid_rows, None), P(grid_rows, None),
            P(None, seq, "head"), P(None, seq, "head"), P(None, seq, "head"),
            P(seq, "head"), P(seq, "head"), P(seq, "head"),
        ),
        check_vma=False,
    )
```

```python
import jax
import jax.numpy as jnp
from jax import lax
from jax.experimental import pallas as pl
from jax.experimental.pallas import tpu as pltpu
from jax.sharding import Mesh
from jax.sharding import PartitionSpec as P

BF = jnp.bfloat16
F4 = jnp.float32
HD = 128
G = 8
W = G * HD
KB = 512
RB = 512
NEG = -1e30
LIMIT = 55.0
SCALE = HD**-0.5
PARAMS = pltpu.CompilerParams(vmem_limit_bytes=56 * 2**20)
SEQ, LIVE, PROMPT, SOURCE = 1, 2, 4, 4


def nt(a, b):
    return lax.dot_general(a, b, (((1,), (1,)), ((), ())), preferred_element_type=F4)


def nn(a, b):
    return lax.dot_general(a, b, (((1,), (0,)), ((), ())), preferred_element_type=F4)


def cols(g):
    return slice(g * HD, (g + 1) * HD)


def kv_block(kv, which, p, j):
    ring = pl.multiple_of((j & 1) * 8, 8)
    return kv[pl.ds(ring, 8), j >> 1, which, p].reshape(KB, HD)


def causal_mask(seq, j):
    key = j * KB + lax.broadcasted_iota(jnp.int32, (KB, RB), 0)
    row = seq * 64 + (lax.broadcasted_iota(jnp.int32, (KB, RB), 1) & 63)
    return key <= row


def self_mask(j, live_0, width):
    key = lax.broadcasted_iota(jnp.int32, (256, width), 0)
    row = j * 128 + (lax.broadcasted_iota(jnp.int32, (256, width), 1) & 127)
    first = jnp.where(live_0 > 0, 0, j * 128)
    return (key >= first) & (key <= row)


def load_queries(qx, qp, qs, qr):
    for g in range(G):
        for p in range(2):
            at = pl.ds(g * 64, 64)
            qx[p, at, :] = qp[p, :, cols(g)]
            qx[6 + p, at, :] = qr[p * 64 : p * 64 + 64, cols(g)]
        for j in range(2):
            at = pl.ds((g % 4) * 128, 128)
            qx[2 + 2 * j + g // 4, at, :] = qs[j * 128 : j * 128 + 128, cols(g)]
            qx[8 + 2 * j + g // 4, at, :] = qr[128 + j * 128 : 256 + j * 128, cols(g)]


def load_own_pairs(kx, ks, vs, qr):
    for which, ref in ((0, ks), (1, vs)):
        kx[0, which] = ref[...]
        for n in range(4):
            kx[1, which, n * 64 : n * 64 + 64, :] = qr[384:448, cols(which * 4 + n)]


def step(k, q, vt, m, l, acc, mask=None):
    s = nt(k, q)
    if mask is not None:
        s = jnp.where(mask, s, NEG)
    top = jnp.maximum(m, jnp.max(s, 0, keepdims=True))
    p = jnp.exp((s - top) * SCALE).astype(BF)
    fade = jnp.exp((m - top) * SCALE)
    l = l * fade + jnp.sum(p.astype(F4), 0, keepdims=True)
    return top, l, acc * fade + nn(vt, p)


def small_step(k, q, vt, m, l, acc, mask=None):
    p = jnp.exp(nt(k, q) * SCALE)
    if mask is not None:
        p = jnp.where(mask, p, 0.0)
    p = p.astype(BF)
    return m, l + jnp.sum(p.astype(F4), 0, keepdims=True), acc + nn(vt, p)


def top_norm(blocks):
    ones = jnp.ones((8, HD), BF)
    top = jnp.zeros((8, 1), F4)
    for block in blocks:
        top = jnp.maximum(top, jnp.max(nt(ones, block * block), 1, keepdims=True))
    return jnp.max(top)


def fwd_kernel(info, kv, ks, vs, qp, qs, qr, o, ot, lse, vt, qx, kx, vst):
    load_queries(qx, qp, qs, qr)
    load_own_pairs(kx, ks, vs, qr)
    keys = [kv_block(kv, 0, p, j) for p in range(2) for j in range(4)] + [kx[0, 0], kx[1, 0]]
    limit = top_norm([qx[n] for n in range(12)]) * top_norm(keys) * (1.05 * SCALE * SCALE)
    args = (info, kv, qx, kx, o, ot, lse, vt, vst)

    @pl.when(limit < LIMIT * LIMIT)
    def _():
        fwd_rows(small_step, 0.0, *args)

    @pl.when(jnp.logical_not(limit < LIMIT * LIMIT))
    def _():
        fwd_rows(step, NEG, *args)


def fwd_rows(step, start, info, kv, qx, kx, o, ot, lse, vt, vst):
    for p in range(2):
        for j in range(4):
            vt[p, j] = kv_block(kv, 1, p, j).T
    for b in range(2):
        vst[b] = kx[b, 1].T
    m0 = jnp.full((1, RB), start, F4)
    l0 = jnp.zeros((1, RB), F4)

    def finish(at, m, l, acc):
        acc = acc * (1.0 / l)
        ot[at] = acc
        lse[at] = m * SCALE + jnp.log(l)
        return acc.T.astype(BF)

    def prompts(b, carry):
        seq = info[SEQ + SOURCE * b]
        group = (info[0] ^ b) * 4
        last = seq >> 3
        for p in range(2):
            ot[6 * b + p] = jnp.zeros((HD, RB), F4)

        def body(j, c, masked=False):
            mask = causal_mask(seq, j) if masked else None
            out = []
            for p in range(2):
                m, l, acc = step(
                    kv_block(kv, 0, p, j), qx[6 * b + p], vt[p, j],
                    c[2 * p], c[2 * p + 1], ot[6 * b + p], mask,
                )
                ot[6 * b + p] = acc
                out += [m, l]
            return tuple(out)

        c = lax.fori_loop(0, last, body, (m0, l0, m0, l0))
        c = body(last, c, True)
        for p in range(2):
            rows = finish(6 * b + p, c[2 * p], c[2 * p + 1], ot[6 * b + p])
            for g in range(G):
                o[pl.ds(group, 4), p * 16 : p * 16 + 16, cols(g)] = rows[
                    g * 64 : g * 64 + 64
                ].reshape(4, 16, HD)
        return carry

    lax.fori_loop(0, 2, prompts, 0)

    def slots(n, carry):
        b, j = n >> 1, n & 1
        live = info[SEQ + SOURCE * b + 1 + j]
        live_0 = info[SEQ + SOURCE * b + 1]
        prompt = info[SEQ + SOURCE * b + 3]
        group = (info[0] ^ b) * 4 + 2 * j
        at = 6 * b + 2 + 2 * j

        @pl.when(live > 0)
        def _():
            q = qx[pl.ds(at, 2)].reshape(2 * RB, HD)
            m, l = jnp.full((1, 2 * RB), start, F4), jnp.zeros((1, 2 * RB), F4)
            acc = jnp.zeros((HD, 2 * RB), F4)
            for kb in range(4):
                m, l, acc = step(kv_block(kv, 0, prompt, kb), q, vt[prompt, kb], m, l, acc)
            m, l, acc = step(kx[b, 0], q, vst[b], m, l, acc, mask=self_mask(j, live_0, 2 * RB))
            total = m * SCALE + jnp.log(l)
            acc = acc * (1.0 / l)
            for h in range(2):
                ot[at + h] = acc[:, h * RB : h * RB + RB]
                lse[at + h] = total[:, h * RB : h * RB + RB]
            rows = acc.T.astype(BF)
            for g in range(G):
                o[pl.ds(group, 2), 32:96, cols(g)] = rows[g * 128 : g * 128 + 128].reshape(
                    2, 64, HD
                )

        @pl.when(live == 0)
        def _():
            o[pl.ds(group, 2), 32:96, :] = jnp.zeros((2, 64, W), BF)

        return carry

    lax.fori_loop(0, 4, slots, 0)


def grads(k, v, q, do, kt, total, delta, mask=None):
    s = nt(k, q)
    dp = nt(v, do)
    e = s * SCALE - total
    if mask is not None:
        e = jnp.where(mask, e, NEG)
    p = jnp.exp(e)
    ds = (p * (dp - delta)).astype(BF)
    return nn(p.astype(BF), do), nn(ds, q), nn(kt, ds)


def bwd_kernel(
    info, kv, ks, vs, qp, qs, qr, do, ot, lse,
    tab, dqp, dqs, drk, drv, send, kt, qx, dx, kx, kst, dk, dv, dqt, dkx, dvx,
):
    load_queries(qx, qp, qs, qr)
    load_own_pairs(kx, ks, vs, qr)
    for b in range(2):
        group = (info[0] ^ b) * 4
        for g in range(G):
            for p in range(2):
                dx[6 * b + p, g * 64 : g * 64 + 64, :] = do[
                    pl.ds(group, 4), p * 16 : p * 16 + 16, cols(g)
                ].reshape(64, HD)
            for j in range(2):
                dx[6 * b + 2 + 2 * j + g // 4, (g % 4) * 128 : (g % 4) * 128 + 128, :] = do[
                    pl.ds(group + 2 * j, 2), 32:96, cols(g)
                ].reshape(128, HD)
        kst[b] = kx[b, 0].T
    for p in range(2):
        for j in range(4):
            kt[p, j] = kv_block(kv, 0, p, j).T
    for ref in (dk, dv, dkx, dvx):
        ref[...] = jnp.zeros_like(ref)

    def row_delta(at):
        return jnp.sum(dx[at].astype(F4).T * ot[at], 0, keepdims=True)

    def prompts(b, carry):
        seq = info[SEQ + SOURCE * b]
        last = seq >> 3
        delta = [row_delta(6 * b + p) for p in range(2)]
        for p in range(2):
            dqt[6 * b + p] = jnp.zeros((HD, RB), F4)

        def body(j, c, masked=False):
            mask = causal_mask(seq, j) if masked else None
            for p in range(2):
                at = 6 * b + p
                a_v, a_k, a_q = grads(
                    kv_block(kv, 0, p, j), kv_block(kv, 1, p, j), qx[at], dx[at], kt[p, j],
                    lse[at], delta[p], mask,
                )
                dv[p, j] += a_v
                dk[p, j] += a_k
                dqt[at] += a_q
            return c

        lax.fori_loop(0, last, body, 0)
        body(last, 0, True)
        return carry

    lax.fori_loop(0, 2, prompts, 0)

    def slots(n, carry):
        b, j = n >> 1, n & 1
        live = info[SEQ + SOURCE * b + 1 + j]
        live_0 = info[SEQ + SOURCE * b + 1]
        prompt = info[SEQ + SOURCE * b + 3]

        @pl.when(live > 0)
        def _():
            mask = self_mask(j, live_0, RB)
            for h in range(2):
                at = 6 * b + 2 + 2 * j + h
                q, d, total = qx[at], dx[at], lse[at]
                delta = row_delta(at)
                acc = jnp.zeros((HD, RB), F4)
                for kb in range(4):
                    a_v, a_k, a_q = grads(
                        kv_block(kv, 0, prompt, kb), kv_block(kv, 1, prompt, kb), q, d,
                        kt[prompt, kb], total, delta,
                    )
                    dv[prompt, kb] += a_v
                    dk[prompt, kb] += a_k
                    acc = acc + a_q
                a_v, a_k, a_q = grads(kx[b, 0], kx[b, 1], q, d, kst[b], total, delta, mask)
                dvx[b] += a_v
                dkx[b] += a_k
                dqt[at] = acc + a_q

        @pl.when(live == 0)
        def _():
            for h in range(2):
                dqt[6 * b + 2 + 2 * j + h] = jnp.zeros((HD, RB), F4)

        return carry

    lax.fori_loop(0, 4, slots, 0)
    for b in range(2):
        for p in range(2):
            rows = (dqt[6 * b + p] * SCALE).T
            for g in range(G):
                part = rows[g * 64 : g * 64 + 64]
                if b == 0:
                    dqp[p, :, cols(g)] = part
                else:
                    send[p * 64 : p * 64 + 64, cols(g)] = part.astype(BF)
        for n in range(4):
            rows = (dqt[6 * b + 2 + n] * SCALE).T
            j, h = n // 2, n % 2
            for g in range(4):
                part = rows[g * 128 : g * 128 + 128]
                if b == 0:
                    dqs[j * 128 : j * 128 + 128, cols(4 * h + g)] = part
                else:
                    send[128 + j * 128 : 256 + j * 128, cols(4 * h + g)] = part.astype(BF)
    drk[...] = dkx[0] * SCALE
    drv[...] = dvx[0]
    for n in range(4):
        send[384:448, cols(n)] = (dkx[1, n * 64 : n * 64 + 64, :] * SCALE).astype(BF)
        send[384:448, cols(4 + n)] = dvx[1, n * 64 : n * 64 + 64, :].astype(BF)
    for p in range(2):
        for j in range(4):
            ring = (j & 1) * 8
            tab[ring : ring + 8, j >> 1, 0, p] = (dk[p, j] * SCALE).astype(BF).reshape(8, 64, HD)
            tab[ring : ring + 8, j >> 1, 1, p] = dv[p, j].astype(BF).reshape(8, 64, HD)


def whole(shape):
    return pl.BlockSpec(tuple(shape), lambda i, info: (0,) * len(shape))


def half_of(shape, other=0):
    lead = (0,) * (len(shape) - 1)
    return pl.BlockSpec(tuple(shape), lambda i, info: lead + (info[0] ^ other,))


ANY = pl.BlockSpec(memory_space=pl.ANY)


def call(kernel, info, ins, in_specs, outs, out_specs, scratch=(), grid=(1,), flops=0, aliases=None):
    name = kernel.__name__.replace("_kernel", "")
    return pl.pallas_call(
        kernel,
        grid_spec=pltpu.PrefetchScalarGridSpec(
            num_scalar_prefetch=1, grid=grid, in_specs=in_specs, out_specs=out_specs,
            scratch_shapes=list(scratch),
        ),
        out_shape=[jax.ShapeDtypeStruct(shape, dtype) for shape, dtype in outs],
        input_output_aliases=aliases or {},
        cost_estimate=pl.CostEstimate(
            flops=flops, bytes_accessed=4 * 10**6, transcendentals=flops // 1000
        ),
        compiler_params=PARAMS,
        name=name,
    )(info, *ins)


PACK = (384 + 64, W)
ROWS = [half_of((256, HD)), half_of((256, HD)), half_of((2, 64, W)), half_of((256, W)), whole(PACK)]
STATE = [((12, HD, RB), F4), ((12, 1, RB), F4)]


def fwd(info, kv, rows):
    return call(
        fwd_kernel, info, (kv, *rows), [whole(kv.shape), *ROWS],
        [((8, 96, W), BF), *STATE],
        [whole((8, 96, W)), *(whole(shape) for shape, _ in STATE)],
        [
            pltpu.VMEM((2, 4, HD, KB), BF), pltpu.VMEM((12, RB, HD), BF),
            pltpu.VMEM((2, 2, 256, HD), BF), pltpu.VMEM((2, HD, 256), BF),
        ],
        flops=2 * 10**10,
    )


def bwd(info, kv, rows, cot, out_t, lse):
    return call(
        bwd_kernel, info, (kv, *rows, cot, out_t, lse),
        [whole(kv.shape), *ROWS, whole(cot.shape), *(whole(shape) for shape, _ in STATE)],
        [
            (kv.shape, BF), ((2, 64, 2 * W), F4), ((256, 2 * W), F4),
            ((256, 2 * HD), F4), ((256, 2 * HD), F4), (PACK, BF),
        ],
        [
            whole(kv.shape), half_of((2, 64, W)), half_of((256, W)), half_of((256, HD)),
            half_of((256, HD)), whole(PACK),
        ],
        [
            pltpu.VMEM((2, 4, HD, KB), BF), pltpu.VMEM((12, RB, HD), BF),
            pltpu.VMEM((12, RB, HD), BF), pltpu.VMEM((2, 2, 256, HD), BF),
            pltpu.VMEM((2, HD, 256), BF), pltpu.VMEM((2, 4, KB, HD), F4),
            pltpu.VMEM((2, 4, KB, HD), F4), pltpu.VMEM((12, HD, RB), F4),
            pltpu.VMEM((2, 256, HD), F4), pltpu.VMEM((2, 256, HD), F4),
        ],
        flops=4 * 10**10,
    )


def pick_kv_kernel(info, k, v, out):
    out[0] = k[...]
    out[1] = v[...]


def pick_kv(info, prompt_k, prompt_v):
    return call(
        pick_kv_kernel, info, (prompt_k, prompt_v), [half_of((2, 64, HD), 1)] * 2,
        [((2, 2, 64, HD), BF)], [whole((2, 2, 64, HD))],
    )[0]


def spread_kv_kernel(info, k, v, other, out):
    own = info[0]
    mine = jnp.stack([k[...], v[...]])
    theirs = other[...]
    for dest in range(out.shape[0]):
        out[dest, own] = mine
        out[dest, 1 - own] = theirs


def spread_kv(info, prompt_k, prompt_v, other, ring):
    shape = (ring, 2, 2, 2, 64, HD)
    return call(
        spread_kv_kernel, info, (prompt_k, prompt_v, other),
        [half_of((2, 64, HD))] * 2 + [whole((2, 2, 64, HD))],
        [(shape, BF)], [whole(shape)],
    )[0]


def pick_rows_kernel(info, qp, qs, ks, vs, out):
    out[:128] = qp[...].reshape(128, W)
    out[128:384] = qs[...]
    for n in range(4):
        out[384:448, cols(n)] = ks[n * 64 : n * 64 + 64, :]
        out[384:448, cols(4 + n)] = vs[n * 64 : n * 64 + 64, :]


def pick_rows(info, prompt_q, resp_q, resp_k, resp_v):
    return call(
        pick_rows_kernel, info, (prompt_q, resp_q, resp_k, resp_v),
        [half_of((2, 64, W), 1), half_of((256, W), 1), half_of((256, HD), 1), half_of((256, HD), 1)],
        [(PACK, BF)], [whole(PACK)],
    )[0]


def column(i):
    return 2 * (i % 4) + i // 4


def split_cot_kernel(info, dp, dr, out):
    out[0, :32] = dp[...].reshape(32, W)
    out[0, 32:] = dr[...]


def split_cot(info, d_prompt, d_resp):
    return call(
        split_cot_kernel, info, (d_prompt, d_resp),
        [
            pl.BlockSpec((2, 16, W), lambda i, info: (0, 0, column(i))),
            pl.BlockSpec((64, W), lambda i, info: (0, column(i))),
        ],
        [((8, 96, W), BF)], [pl.BlockSpec((1, 96, W), lambda i, info: (i, 0, 0))], grid=(8,),
    )[0]


def place_out_kernel(info, piece, prompt_out, resp_out):
    prompt_out[...] = piece[0, :32].astype(F4).reshape(2, 16, W)
    resp_out[...] = piece[0, 32:].astype(F4)


def place_out(info, pieces):
    return call(
        place_out_kernel, info, (pieces,),
        [pl.BlockSpec((1, 96, W), lambda i, info: (i, 0, 0))],
        [((2, 16, 8 * W), F4), ((64, 8 * W), F4)],
        [
            pl.BlockSpec((2, 16, W), lambda i, info: (0, 0, column(i))),
            pl.BlockSpec((64, W), lambda i, info: (0, column(i))),
        ],
        grid=(8,),
    )


def place_rows_kernel(info, pack, *refs):
    dqp, dqs, drk, drv = refs[4:]
    dqp[...] = pack[:128].astype(F4).reshape(2, 64, W)
    dqs[...] = pack[128:384].astype(F4)
    for n in range(4):
        drk[n * 64 : n * 64 + 64, :] = pack[384:448, cols(n)].astype(F4)
        drv[n * 64 : n * 64 + 64, :] = pack[384:448, cols(4 + n)].astype(F4)


def place_rows(info, pack, parts):
    return call(
        place_rows_kernel, info, (pack, *parts), [whole(PACK)] + [ANY] * 4,
        [(part.shape, F4) for part in parts],
        [half_of((2, 64, W), 1), half_of((256, W), 1), half_of((256, HD), 1), half_of((256, HD), 1)],
        aliases={2: 0, 3: 1, 4: 2, 5: 3},
    )


def sum_terms_kernel(info, terms, out):
    total = terms[0, 0].astype(F4)
    for source in range(1, terms.shape[0]):
        total = total + terms[source, 0].astype(F4)
    out[...] = total


def sum_terms(info, terms, other):
    shape = (2, 2, 64, HD)
    block = (terms.shape[0], 1, *shape)
    return call(
        sum_terms_kernel, info, (terms,),
        [pl.BlockSpec(block, lambda i, info: (0, info[0] ^ other, 0, 0, 0, 0))],
        [(shape, F4)], [whole(shape)],
    )[0]


def place_kv_kernel(info, own, other, dk, dv):
    start = pl.multiple_of(info[0] * HD, HD)
    rest = pl.multiple_of((1 - info[0]) * HD, HD)
    for which, ref in ((0, dk), (1, dv)):
        ref[:, :, pl.ds(start, HD)] = own[which]
        ref[:, :, pl.ds(rest, HD)] = other[which]


def place_kv(info, own, other):
    shape = (2, 64, 2 * HD)
    return call(
        place_kv_kernel, info, (own, other), [whole(own.shape)] * 2,
        [(shape, F4)] * 2, [whole(shape)] * 2,
    )


def slot_state(slot_resp, resp_len, resp_prompt):
    same = (slot_resp[0] == slot_resp[1]).astype(jnp.int32)
    block = jnp.stack([jnp.zeros((), jnp.int32), same])
    live = ((slot_resp < 1) & (block < resp_len[0])).astype(jnp.int32)
    seq = lax.axis_index(("half", "ring")).astype(jnp.int32)
    return jnp.stack([seq, live[0], live[1], resp_prompt[0]])


def exchange(array, axis):
    return lax.all_to_all(array, axis, split_axis=0, concat_axis=0, tiled=True)


def swap(array):
    return lax.ppermute(array, "half", [(0, 1), (1, 0)])


def after(array, earlier):
    return lax.optimization_barrier((array, earlier))[0]


def shards(
    prompt_q, prompt_k, prompt_v, resp_q, resp_k, resp_v, slot_resp, resp_len, resp_prompt,
    d_prompt_out, d_resp_out,
):
    ring = lax.axis_size("ring")
    half = lax.axis_index("half").astype(jnp.int32).reshape(1)
    kv_other = swap(pick_kv(half, prompt_k, prompt_v))
    kv = exchange(spread_kv(half, prompt_k, prompt_v, kv_other, ring), "ring")
    state = slot_state(slot_resp, resp_len, resp_prompt)
    state_other = swap(state)
    rows_out, state_other = lax.optimization_barrier(
        (pick_rows(half, prompt_q, resp_q, resp_k, resp_v), state_other)
    )
    rows_other = swap(rows_out)
    info = jnp.concatenate([half, state, state_other])
    rows = (resp_k, resp_v, prompt_q, resp_q, rows_other)
    cot = exchange(after(split_cot(half, d_prompt_out, d_resp_out), kv), ("half", "head"))
    pieces, out_t, lse = fwd(info, kv, rows)
    pieces = exchange(pieces, ("half", "head"))
    table, *own_rows, pack = bwd(info, kv, rows, cot, out_t, lse)
    table, pieces = lax.optimization_barrier((table, pieces))
    terms = exchange(table, "ring")
    pack, outs = lax.optimization_barrier((swap(pack), place_out(half, pieces)))
    done = (*outs, *place_rows(half, pack, own_rows))
    terms, done = lax.optimization_barrier((terms, done))
    prompt_out, resp_out, d_prompt_q, d_resp_q, d_resp_k, d_resp_v = done
    send_kv = swap(sum_terms(half, terms, 1))
    own_kv = sum_terms(half, terms, 0)
    d_prompt_k, d_prompt_v = place_kv(half, own_kv, send_kv)
    return (
        prompt_out, resp_out, d_prompt_q, d_prompt_k, d_prompt_v, d_resp_q, d_resp_k, d_resp_v,
    )


def solution(mesh):
    n_seq, n_head = mesh.devices.shape
    fine = Mesh(mesh.devices.reshape(2, n_seq // 2, n_head), ("half", "ring", "head"))
    seq = ("half", "ring")
    grid_rows = (*seq, "head")
    placed = (
        P(None, seq, "head"), P(None, seq, "head"), P(None, seq, "head"),
        P(seq, "head"), P(seq, "head"), P(seq, "head"),
        P(seq), P(seq), P(seq),
        P(None, grid_rows, None), P(grid_rows, None),
    )
    return jax.shard_map(
        shards,
        mesh=fine,
        in_specs=placed,
        out_specs=(
            P(None, grid_rows, None), P(grid_rows, None),
            P(None, seq, "head"), P(None, seq, "head"), P(None, seq, "head"),
            P(seq, "head"), P(seq, "head"), P(seq, "head"),
        ),
        check_vma=False,
    )
```

```python
import jax
import jax.numpy as jnp
from jax import lax
from jax.experimental import pallas as pl
from jax.experimental.pallas import tpu as pltpu
from jax.sharding import Mesh
from jax.sharding import PartitionSpec as P

BF = jnp.bfloat16
F4 = jnp.float32
HD = 128
G = 8
W = G * HD
KB = 512
RB = 512
NEG = -1e30
LIMIT = 55.0
SCALE = HD**-0.5
PARAMS = pltpu.CompilerParams(vmem_limit_bytes=62 * 2**20)
SEQ, LIVE, PROMPT, SOURCE = 1, 2, 4, 4


def nt(a, b):
    return lax.dot_general(a, b, (((1,), (1,)), ((), ())), preferred_element_type=F4)


def nn(a, b):
    return lax.dot_general(a, b, (((1,), (0,)), ((), ())), preferred_element_type=F4)


def cols(g):
    return slice(g * HD, (g + 1) * HD)


def kv_block(kv, which, p, j):
    ring = pl.multiple_of((j & 1) * 8, 8)
    return kv[pl.ds(ring, 8), j >> 1, which, p].reshape(KB, HD)


def causal_mask(seq, j):
    key = j * KB + lax.broadcasted_iota(jnp.int32, (KB, RB), 0)
    row = seq * 64 + (lax.broadcasted_iota(jnp.int32, (KB, RB), 1) & 63)
    return key <= row


def self_mask(j, live_0, width):
    key = lax.broadcasted_iota(jnp.int32, (256, width), 0)
    row = j * 128 + (lax.broadcasted_iota(jnp.int32, (256, width), 1) & 127)
    first = jnp.where(live_0 > 0, 0, j * 128)
    return (key >= first) & (key <= row)


def load_queries(qx, qp, qs, qr):
    for g in range(G):
        for p in range(2):
            at = pl.ds(g * 64, 64)
            qx[p, at, :] = qp[p, :, cols(g)]
            qx[6 + p, at, :] = qr[p * 64 : p * 64 + 64, cols(g)]
        for j in range(2):
            at = pl.ds((g % 4) * 128, 128)
            qx[2 + 2 * j + g // 4, at, :] = qs[j * 128 : j * 128 + 128, cols(g)]
            qx[8 + 2 * j + g // 4, at, :] = qr[128 + j * 128 : 256 + j * 128, cols(g)]


def load_own_pairs(kx, ks, vs, qr):
    for which, ref in ((0, ks), (1, vs)):
        kx[0, which] = ref[...]
        for n in range(4):
            kx[1, which, n * 64 : n * 64 + 64, :] = qr[384:448, cols(which * 4 + n)]


def step(k, q, vt, m, l, acc, mask=None):
    s = nt(k, q)
    if mask is not None:
        s = jnp.where(mask, s, NEG)
    top = jnp.maximum(m, jnp.max(s, 0, keepdims=True))
    p = jnp.exp((s - top) * SCALE).astype(BF)
    fade = jnp.exp((m - top) * SCALE)
    l = l * fade + jnp.sum(p.astype(F4), 0, keepdims=True)
    return top, l, acc * fade + nn(vt, p)


def small_step(k, q, vt, m, l, acc, mask=None):
    p = jnp.exp(nt(k, q) * SCALE)
    if mask is not None:
        p = jnp.where(mask, p, 0.0)
    p = p.astype(BF)
    return m, l + jnp.sum(p.astype(F4), 0, keepdims=True), acc + nn(vt, p)


def top_norm(blocks):
    ones = jnp.ones((8, HD), BF)
    top = jnp.zeros((8, 1), F4)
    for block in blocks:
        top = jnp.maximum(top, jnp.max(nt(ones, block * block), 1, keepdims=True))
    return jnp.max(top)


def fwd_kernel(info, kv, ks, vs, qp, qs, qr, o, ot, lse, vt, qx, kx, vst):
    load_queries(qx, qp, qs, qr)
    load_own_pairs(kx, ks, vs, qr)
    keys = [kv_block(kv, 0, p, j) for p in range(2) for j in range(4)] + [kx[0, 0], kx[1, 0]]
    limit = top_norm([qx[n] for n in range(12)]) * top_norm(keys) * (1.05 * SCALE * SCALE)
    args = (info, kv, qx, kx, o, ot, lse, vt, vst)

    @pl.when(limit < LIMIT * LIMIT)
    def _():
        fwd_rows(small_step, 0.0, *args)

    @pl.when(jnp.logical_not(limit < LIMIT * LIMIT))
    def _():
        fwd_rows(step, NEG, *args)


def fwd_rows(step, start, info, kv, qx, kx, o, ot, lse, vt, vst):
    for p in range(2):
        for j in range(4):
            vt[p, j] = kv_block(kv, 1, p, j).T
    for b in range(2):
        vst[b] = kx[b, 1].T
    m0 = jnp.full((1, RB), start, F4)
    l0 = jnp.zeros((1, RB), F4)

    def finish(at, m, l, acc):
        acc = acc * (1.0 / l)
        ot[at] = acc
        lse[at] = m * SCALE + jnp.log(l)
        return acc.T.astype(BF)

    def prompts(b, carry):
        seq = info[SEQ + SOURCE * b]
        group = (info[0] ^ b) * 4
        last = seq >> 3
        for p in range(2):
            ot[6 * b + p] = jnp.zeros((HD, RB), F4)

        def body(j, c, masked=False):
            mask = causal_mask(seq, j) if masked else None
            out = []
            for p in range(2):
                m, l, acc = step(
                    kv_block(kv, 0, p, j), qx[6 * b + p], vt[p, j],
                    c[2 * p], c[2 * p + 1], ot[6 * b + p], mask,
                )
                ot[6 * b + p] = acc
                out += [m, l]
            return tuple(out)

        c = lax.fori_loop(0, last, body, (m0, l0, m0, l0))
        c = body(last, c, True)
        for p in range(2):
            rows = finish(6 * b + p, c[2 * p], c[2 * p + 1], ot[6 * b + p])
            for g in range(G):
                o[pl.ds(group, 4), p * 16 : p * 16 + 16, cols(g)] = rows[
                    g * 64 : g * 64 + 64
                ].reshape(4, 16, HD)
        return carry

    lax.fori_loop(0, 2, prompts, 0)

    def slots(n, carry):
        b, j = n >> 1, n & 1
        live = info[SEQ + SOURCE * b + 1 + j]
        live_0 = info[SEQ + SOURCE * b + 1]
        prompt = info[SEQ + SOURCE * b + 3]
        group = (info[0] ^ b) * 4 + 2 * j
        at = 6 * b + 2 + 2 * j

        @pl.when(live > 0)
        def _():
            q = qx[pl.ds(at, 2)].reshape(2 * RB, HD)
            m, l = jnp.full((1, 2 * RB), start, F4), jnp.zeros((1, 2 * RB), F4)
            acc = jnp.zeros((HD, 2 * RB), F4)
            for kb in range(4):
                m, l, acc = step(kv_block(kv, 0, prompt, kb), q, vt[prompt, kb], m, l, acc)
            m, l, acc = step(kx[b, 0], q, vst[b], m, l, acc, mask=self_mask(j, live_0, 2 * RB))
            total = m * SCALE + jnp.log(l)
            acc = acc * (1.0 / l)
            for h in range(2):
                ot[at + h] = acc[:, h * RB : h * RB + RB]
                lse[at + h] = total[:, h * RB : h * RB + RB]
            rows = acc.T.astype(BF)
            for g in range(G):
                o[pl.ds(group, 2), 32:96, cols(g)] = rows[g * 128 : g * 128 + 128].reshape(
                    2, 64, HD
                )

        @pl.when(live == 0)
        def _():
            o[pl.ds(group, 2), 32:96, :] = jnp.zeros((2, 64, W), BF)

        return carry

    lax.fori_loop(0, 4, slots, 0)


def grads(k, v, q, do, kt, total, delta, mask=None):
    s = nt(k, q)
    dp = nt(v, do)
    e = s * SCALE - total
    if mask is not None:
        e = jnp.where(mask, e, NEG)
    p = jnp.exp(e)
    ds = (p * (dp - delta)).astype(BF)
    return nn(p.astype(BF), do), nn(ds, q), nn(kt, ds)


def bwd_kernel(
    info, kv, ks, vs, qp, qs, qr, do, ot, lse,
    tab, dqp, dqs, drk, drv, send, kt, qx, dx, kx, kst, dk, dv, dqt, dkx, dvx,
):
    load_queries(qx, qp, qs, qr)
    load_own_pairs(kx, ks, vs, qr)
    for b in range(2):
        group = (info[0] ^ b) * 4
        for g in range(G):
            for p in range(2):
                dx[6 * b + p, g * 64 : g * 64 + 64, :] = do[
                    pl.ds(group, 4), p * 16 : p * 16 + 16, cols(g)
                ].reshape(64, HD)
            for j in range(2):
                dx[6 * b + 2 + 2 * j + g // 4, (g % 4) * 128 : (g % 4) * 128 + 128, :] = do[
                    pl.ds(group + 2 * j, 2), 32:96, cols(g)
                ].reshape(128, HD)
        kst[b] = kx[b, 0].T
    for p in range(2):
        for j in range(4):
            kt[p, j] = kv_block(kv, 0, p, j).T
    for ref in (dk, dv, dkx, dvx):
        ref[...] = jnp.zeros_like(ref)

    def row_delta(at):
        return jnp.sum(dx[at].astype(F4).T * ot[at], 0, keepdims=True)

    def prompts(b, carry):
        seq = info[SEQ + SOURCE * b]
        last = seq >> 3
        delta = [row_delta(6 * b + p) for p in range(2)]
        for p in range(2):
            dqt[6 * b + p] = jnp.zeros((HD, RB), F4)

        def body(j, c, masked=False):
            mask = causal_mask(seq, j) if masked else None
            for p in range(2):
                at = 6 * b + p
                a_v, a_k, a_q = grads(
                    kv_block(kv, 0, p, j), kv_block(kv, 1, p, j), qx[at], dx[at], kt[p, j],
                    lse[at], delta[p], mask,
                )
                dv[p, j] += a_v
                dk[p, j] += a_k
                dqt[at] += a_q
            return c

        lax.fori_loop(0, last, body, 0)
        body(last, 0, True)
        return carry

    lax.fori_loop(0, 2, prompts, 0)

    def slots(n, carry):
        b, j = n >> 1, n & 1
        live = info[SEQ + SOURCE * b + 1 + j]
        live_0 = info[SEQ + SOURCE * b + 1]
        prompt = info[SEQ + SOURCE * b + 3]

        @pl.when(live > 0)
        def _():
            mask = self_mask(j, live_0, RB)
            for h in range(2):
                at = 6 * b + 2 + 2 * j + h
                q, d, total = qx[at], dx[at], lse[at]
                delta = row_delta(at)
                acc = jnp.zeros((HD, RB), F4)
                for kb in range(4):
                    a_v, a_k, a_q = grads(
                        kv_block(kv, 0, prompt, kb), kv_block(kv, 1, prompt, kb), q, d,
                        kt[prompt, kb], total, delta,
                    )
                    dv[prompt, kb] += a_v
                    dk[prompt, kb] += a_k
                    acc = acc + a_q
                a_v, a_k, a_q = grads(kx[b, 0], kx[b, 1], q, d, kst[b], total, delta, mask)
                dvx[b] += a_v
                dkx[b] += a_k
                dqt[at] = acc + a_q

        @pl.when(live == 0)
        def _():
            for h in range(2):
                dqt[6 * b + 2 + 2 * j + h] = jnp.zeros((HD, RB), F4)

        return carry

    lax.fori_loop(0, 4, slots, 0)
    for b in range(2):
        for p in range(2):
            rows = (dqt[6 * b + p] * SCALE).T
            for g in range(G):
                part = rows[g * 64 : g * 64 + 64]
                if b == 0:
                    dqp[p, :, cols(g)] = part
                else:
                    send[p * 64 : p * 64 + 64, cols(g)] = part.astype(BF)
        for n in range(4):
            rows = (dqt[6 * b + 2 + n] * SCALE).T
            j, h = n // 2, n % 2
            for g in range(4):
                part = rows[g * 128 : g * 128 + 128]
                if b == 0:
                    dqs[j * 128 : j * 128 + 128, cols(4 * h + g)] = part
                else:
                    send[128 + j * 128 : 256 + j * 128, cols(4 * h + g)] = part.astype(BF)
    drk[...] = dkx[0] * SCALE
    drv[...] = dvx[0]
    for n in range(4):
        send[384:448, cols(n)] = (dkx[1, n * 64 : n * 64 + 64, :] * SCALE).astype(BF)
        send[384:448, cols(4 + n)] = dvx[1, n * 64 : n * 64 + 64, :].astype(BF)
    for p in range(2):
        for j in range(4):
            ring = (j & 1) * 8
            tab[ring : ring + 8, j >> 1, 0, p] = (dk[p, j] * SCALE).astype(BF).reshape(8, 64, HD)
            tab[ring : ring + 8, j >> 1, 1, p] = dv[p, j].astype(BF).reshape(8, 64, HD)


def whole(shape):
    return pl.BlockSpec(tuple(shape), lambda i, info: (0,) * len(shape))


def half_of(shape, other=0):
    lead = (0,) * (len(shape) - 1)
    return pl.BlockSpec(tuple(shape), lambda i, info: lead + (info[0] ^ other,))


ANY = pl.BlockSpec(memory_space=pl.ANY)


def call(kernel, info, ins, in_specs, outs, out_specs, scratch=(), grid=(1,), flops=0, aliases=None):
    name = kernel.__name__.replace("_kernel", "")
    return pl.pallas_call(
        kernel,
        grid_spec=pltpu.PrefetchScalarGridSpec(
            num_scalar_prefetch=1, grid=grid, in_specs=in_specs, out_specs=out_specs,
            scratch_shapes=list(scratch),
        ),
        out_shape=[jax.ShapeDtypeStruct(shape, dtype) for shape, dtype in outs],
        input_output_aliases=aliases or {},
        cost_estimate=pl.CostEstimate(
            flops=flops, bytes_accessed=4 * 10**6, transcendentals=flops // 1000
        ),
        compiler_params=PARAMS,
        name=name,
    )(info, *ins)


PACK = (384 + 64, W)
ROWS = [half_of((256, HD)), half_of((256, HD)), half_of((2, 64, W)), half_of((256, W)), whole(PACK)]
STATE = [((12, HD, RB), F4), ((12, 1, RB), F4)]


def fwd(info, kv, rows):
    return call(
        fwd_kernel, info, (kv, *rows), [whole(kv.shape), *ROWS],
        [((8, 96, W), BF), *STATE],
        [whole((8, 96, W)), *(whole(shape) for shape, _ in STATE)],
        [
            pltpu.VMEM((2, 4, HD, KB), BF), pltpu.VMEM((12, RB, HD), BF),
            pltpu.VMEM((2, 2, 256, HD), BF), pltpu.VMEM((2, HD, 256), BF),
        ],
        flops=2 * 10**10,
    )


def bwd(info, kv, rows, cot, out_t, lse):
    return call(
        bwd_kernel, info, (kv, *rows, cot, out_t, lse),
        [whole(kv.shape), *ROWS, whole(cot.shape), *(whole(shape) for shape, _ in STATE)],
        [
            (kv.shape, BF), ((2, 64, 2 * W), F4), ((256, 2 * W), F4),
            ((256, 2 * HD), F4), ((256, 2 * HD), F4), (PACK, BF),
        ],
        [
            whole(kv.shape), half_of((2, 64, W)), half_of((256, W)), half_of((256, HD)),
            half_of((256, HD)), whole(PACK),
        ],
        [
            pltpu.VMEM((2, 4, HD, KB), BF), pltpu.VMEM((12, RB, HD), BF),
            pltpu.VMEM((12, RB, HD), BF), pltpu.VMEM((2, 2, 256, HD), BF),
            pltpu.VMEM((2, HD, 256), BF), pltpu.VMEM((2, 4, KB, HD), F4),
            pltpu.VMEM((2, 4, KB, HD), F4), pltpu.VMEM((12, HD, RB), F4),
            pltpu.VMEM((2, 256, HD), F4), pltpu.VMEM((2, 256, HD), F4),
        ],
        flops=4 * 10**10,
    )


def pick_kv_kernel(info, k, v, out):
    out[0] = k[...]
    out[1] = v[...]


def pick_kv(info, prompt_k, prompt_v):
    return call(
        pick_kv_kernel, info, (prompt_k, prompt_v), [half_of((2, 64, HD), 1)] * 2,
        [((2, 2, 64, HD), BF)], [whole((2, 2, 64, HD))],
    )[0]


def spread_kv_kernel(info, k, v, other, out):
    own = info[0]
    mine = jnp.stack([k[...], v[...]])
    theirs = other[...]
    for dest in range(out.shape[0]):
        out[dest, own] = mine
        out[dest, 1 - own] = theirs


def spread_kv(info, prompt_k, prompt_v, other, ring):
    shape = (ring, 2, 2, 2, 64, HD)
    return call(
        spread_kv_kernel, info, (prompt_k, prompt_v, other),
        [half_of((2, 64, HD))] * 2 + [whole((2, 2, 64, HD))],
        [(shape, BF)], [whole(shape)],
    )[0]


def pick_rows_kernel(info, qp, qs, ks, vs, out):
    out[:128] = qp[...].reshape(128, W)
    out[128:384] = qs[...]
    for n in range(4):
        out[384:448, cols(n)] = ks[n * 64 : n * 64 + 64, :]
        out[384:448, cols(4 + n)] = vs[n * 64 : n * 64 + 64, :]


def pick_rows(info, prompt_q, resp_q, resp_k, resp_v):
    return call(
        pick_rows_kernel, info, (prompt_q, resp_q, resp_k, resp_v),
        [half_of((2, 64, W), 1), half_of((256, W), 1), half_of((256, HD), 1), half_of((256, HD), 1)],
        [(PACK, BF)], [whole(PACK)],
    )[0]


def column(i):
    return 2 * (i % 4) + i // 4


def split_cot_kernel(info, dp, dr, out):
    out[0, :32] = dp[...].reshape(32, W)
    out[0, 32:] = dr[...]


def split_cot(info, d_prompt, d_resp):
    return call(
        split_cot_kernel, info, (d_prompt, d_resp),
        [
            pl.BlockSpec((2, 16, W), lambda i, info: (0, 0, column(i))),
            pl.BlockSpec((64, W), lambda i, info: (0, column(i))),
        ],
        [((8, 96, W), BF)], [pl.BlockSpec((1, 96, W), lambda i, info: (i, 0, 0))], grid=(8,),
    )[0]


def place_out_kernel(info, piece, prompt_out, resp_out):
    prompt_out[...] = piece[0, :32].astype(F4).reshape(2, 16, W)
    resp_out[...] = piece[0, 32:].astype(F4)


def place_out(info, pieces):
    return call(
        place_out_kernel, info, (pieces,),
        [pl.BlockSpec((1, 96, W), lambda i, info: (i, 0, 0))],
        [((2, 16, 8 * W), F4), ((64, 8 * W), F4)],
        [
            pl.BlockSpec((2, 16, W), lambda i, info: (0, 0, column(i))),
            pl.BlockSpec((64, W), lambda i, info: (0, column(i))),
        ],
        grid=(8,),
    )


def place_rows_kernel(info, pack, *refs):
    dqp, dqs, drk, drv = refs[4:]
    dqp[...] = pack[:128].astype(F4).reshape(2, 64, W)
    dqs[...] = pack[128:384].astype(F4)
    for n in range(4):
        drk[n * 64 : n * 64 + 64, :] = pack[384:448, cols(n)].astype(F4)
        drv[n * 64 : n * 64 + 64, :] = pack[384:448, cols(4 + n)].astype(F4)


def place_rows(info, pack, parts):
    return call(
        place_rows_kernel, info, (pack, *parts), [whole(PACK)] + [ANY] * 4,
        [(part.shape, F4) for part in parts],
        [half_of((2, 64, W), 1), half_of((256, W), 1), half_of((256, HD), 1), half_of((256, HD), 1)],
        aliases={2: 0, 3: 1, 4: 2, 5: 3},
    )


def sum_terms_kernel(info, terms, out):
    total = terms[0, 0].astype(F4)
    for source in range(1, terms.shape[0]):
        total = total + terms[source, 0].astype(F4)
    out[...] = total


def sum_terms(info, terms, other):
    shape = (2, 2, 64, HD)
    block = (terms.shape[0], 1, *shape)
    return call(
        sum_terms_kernel, info, (terms,),
        [pl.BlockSpec(block, lambda i, info: (0, info[0] ^ other, 0, 0, 0, 0))],
        [(shape, F4)], [whole(shape)],
    )[0]


def place_kv_kernel(info, own, other, dk, dv):
    start = pl.multiple_of(info[0] * HD, HD)
    rest = pl.multiple_of((1 - info[0]) * HD, HD)
    for which, ref in ((0, dk), (1, dv)):
        ref[:, :, pl.ds(start, HD)] = own[which]
        ref[:, :, pl.ds(rest, HD)] = other[which]


def place_kv(info, own, other):
    shape = (2, 64, 2 * HD)
    return call(
        place_kv_kernel, info, (own, other), [whole(own.shape)] * 2,
        [(shape, F4)] * 2, [whole(shape)] * 2,
    )


def slot_state(slot_resp, resp_len, resp_prompt):
    same = (slot_resp[0] == slot_resp[1]).astype(jnp.int32)
    block = jnp.stack([jnp.zeros((), jnp.int32), same])
    live = ((slot_resp < 1) & (block < resp_len[0])).astype(jnp.int32)
    seq = lax.axis_index(("half", "ring")).astype(jnp.int32)
    return jnp.stack([seq, live[0], live[1], resp_prompt[0]])


def exchange(array, axis):
    return lax.all_to_all(array, axis, split_axis=0, concat_axis=0, tiled=True)


def swap(array):
    return lax.ppermute(array, "half", [(0, 1), (1, 0)])


def after(array, earlier):
    return lax.optimization_barrier((array, earlier))[0]


def shards(
    prompt_q, prompt_k, prompt_v, resp_q, resp_k, resp_v, slot_resp, resp_len, resp_prompt,
    d_prompt_out, d_resp_out,
):
    ring = lax.axis_size("ring")
    half = lax.axis_index("half").astype(jnp.int32).reshape(1)
    kv_other = swap(pick_kv(half, prompt_k, prompt_v))
    kv = exchange(spread_kv(half, prompt_k, prompt_v, kv_other, ring), "ring")
    state = slot_state(slot_resp, resp_len, resp_prompt)
    state_other = swap(state)
    rows_out, state_other = lax.optimization_barrier(
        (pick_rows(half, prompt_q, resp_q, resp_k, resp_v), state_other)
    )
    rows_other = swap(rows_out)
    info = jnp.concatenate([half, state, state_other])
    rows = (resp_k, resp_v, prompt_q, resp_q, rows_other)
    cot = exchange(after(split_cot(half, d_prompt_out, d_resp_out), kv), ("half", "head"))
    pieces, out_t, lse = fwd(info, kv, rows)
    pieces = exchange(pieces, ("half", "head"))
    table, *own_rows, pack = bwd(info, kv, rows, cot, out_t, lse)
    table, pieces = lax.optimization_barrier((table, pieces))
    terms = exchange(table, "ring")
    pack, outs = lax.optimization_barrier((swap(pack), place_out(half, pieces)))
    done = (*outs, *place_rows(half, pack, own_rows))
    terms, done = lax.optimization_barrier((terms, done))
    prompt_out, resp_out, d_prompt_q, d_resp_q, d_resp_k, d_resp_v = done
    send_kv = swap(sum_terms(half, terms, 1))
    own_kv = sum_terms(half, terms, 0)
    d_prompt_k, d_prompt_v = place_kv(half, own_kv, send_kv)
    return (
        prompt_out, resp_out, d_prompt_q, d_prompt_k, d_prompt_v, d_resp_q, d_resp_k, d_resp_v,
    )


def solution(mesh):
    n_seq, n_head = mesh.devices.shape
    fine = Mesh(mesh.devices.reshape(2, n_seq // 2, n_head), ("half", "ring", "head"))
    seq = ("half", "ring")
    grid_rows = (*seq, "head")
    placed = (
        P(None, seq, "head"), P(None, seq, "head"), P(None, seq, "head"),
        P(seq, "head"), P(seq, "head"), P(seq, "head"),
        P(seq), P(seq), P(seq),
        P(None, grid_rows, None), P(grid_rows, None),
    )
    return jax.shard_map(
        shards,
        mesh=fine,
        in_specs=placed,
        out_specs=(
            P(None, grid_rows, None), P(grid_rows, None),
            P(None, seq, "head"), P(None, seq, "head"), P(None, seq, "head"),
            P(seq, "head"), P(seq, "head"), P(seq, "head"),
        ),
        check_vma=False,
    )
```
